32 devices in a mesh: segment: 4 (over y, x), dp: 8 (over z, core).
Axes of the slice: x: 2, y: 2, z: 4, core: 2. Of those that a mesh axis runs over, the one named last changes fastest.
Arguments:
- tokens: bfloat16 [16, 512, 768], P('dp'), may hold values from -6 to 6
- group_ids: int32 [16, 512], P('dp'), may hold values from 0 to 2, as said below
- type_ids: int32 [16, 512], P('dp'), may hold values from 0 to 1, as said below
- norm_gain: bfloat16 [4, 768], P('segment'), may hold values from 0.5 to 1.5
- norm_bias: bfloat16 [4, 768], P('segment'), may hold values from -1.75 to 1.75
- qkv_weight: bfloat16 [2, 768, 2304], replicated, may hold values from -0.21875 to 0.21875
- qv_bias: bfloat16 [2, 2, 768], replicated, may hold values from -1.75 to 1.75
- out_weight: bfloat16 [2, 768, 768], replicated, may hold values from -1.75 to 1.75
- out_bias: bfloat16 [2, 768], replicated, may hold values from -1.75 to 1.75
- up_weight: bfloat16 [3, 768, 3072], replicated, may hold values from -0.21875 to 0.21875
- up_bias: bfloat16 [3, 3072], replicated, may hold values from -1.75 to 1.75
- down_weight: bfloat16 [3, 3072, 768], replicated, may hold values from -0.109375 to 0.109375
- down_bias: bfloat16 [3, 768], replicated, may hold values from -1.75 to 1.75
- out_cotangent: bfloat16 [16, 512, 768], P('dp'), may hold values from -8 to 8
Outputs:
- layer_output: bfloat16 [16, 512, 768], P('dp', 'segment')
- input_grad: float32 [16, 512, 768], P('dp', 'segment')
- norm_gain_grad: float32 [4, 768], P('segment', 'dp')
- norm_bias_grad: float32 [4, 768], P('segment', 'dp')
- qkv_weight_grad: float32 [2, 768, 2304], P(None, 'dp')
- qv_bias_grad: float32 [2, 2, 768], P(None, None, 'dp')
- out_weight_grad: float32 [2, 768, 768], P(None, 'dp')
- out_bias_grad: float32 [2, 768], P(None, 'dp')
- up_weight_grad: float32 [3, 768, 3072], P(None, 'dp')
- up_bias_grad: float32 [3, 3072], P(None, 'dp')
- down_weight_grad: float32 [3, 3072, 768], P(None, 'dp')
- down_bias_grad: float32 [3, 768], P(None, 'dp')
The draws below stay inside these ranges and needn't reach their ends.
Inputs may be any that keep to these rules, and one draw needn't show every extreme that they name: `group_ids`: in each row of 512 tokens the group numbers never fall and all three occur: group 0 is text, group 1 is one item of 197 image tokens followed by 1 to 3 captions of 64 tokens, group 2 is text. `type_ids`: in each row, type 0 marks exactly the first 197 tokens of group 1, one unbroken run; every other token is 1.
All inputs are finite; a program needn't handle non-finite values.
Results may differ from the reference program's by a relative error of at most 0.014.
Values may be sent and summed in bfloat16 or wider, within the bound.
A program may use at most 512 MiB of HBM per device.

```python
import jax
import jax.numpy as jnp
from jax import lax

D = 768
H = 12
HD = 64
FF = 3072
ROWS = 512
PATCHES = 197
CAP = 64
MICRO = 2
LAYERS = 2
SECTIONS = 4
N_DP = 8


def item_layout(key):
    row_total = N_DP * MICRO
    caption_key, leading_key = jax.random.split(key)
    caption_top = min(3, (ROWS - PATCHES - CAP - 1) // CAP)
    captions = jax.random.randint(caption_key, (row_total,), 1, caption_top + 1)
    spare_room = ROWS - PATCHES - CAP * captions
    leading = CAP * jax.random.randint(leading_key, (row_total,), 1, (spare_room - 1) // CAP + 1)
    item_end = leading + PATCHES + CAP * captions
    position = jnp.arange(ROWS, dtype=jnp.int32)[None, :]
    return (leading[:, None].astype(jnp.int32), item_end[:, None].astype(jnp.int32), position)


def draw_group_ids(key, part):
    leading, item_end, position = item_layout(key)
    return (position >= leading).astype(jnp.int32) + (position >= item_end).astype(jnp.int32)


def draw_type_ids(key, part):
    leading, item_end, position = item_layout(key)
    image_mask = (position >= leading) & (position < leading + PATCHES)
    return 1 - image_mask.astype(jnp.int32)


def raised(entries, key, source, target, blocks, factor):
    owner, partner = [(jnp.arange(entries.shape[dim]) // (entries.shape[dim] // blocks)).reshape([-1 if axis == dim else 1 for axis in range(entries.ndim)]) for dim in (source, target)]
    chosen = jax.random.permutation(key, blocks)[partner]
    strong = (owner == chosen) | (owner == (partner + blocks // 2) % blocks)
    return jnp.where(strong, factor * entries, entries)


def block_levels(own_key, shape, shards, smallest, high):
    def one(dim, blocks):
        heights = jax.random.uniform(jax.random.fold_in(jax.random.fold_in(own_key, 6), dim), (blocks,), jnp.float32, smallest / len(shards), high / len(shards))
        return jnp.repeat(jnp.exp(heights), shape[dim] // blocks).reshape((-1,) + (1,) * (len(shape) - dim - 1))

    factor_of = one(*shards[0])
    for cut in shards[1:]:
        factor_of = factor_of * one(*cut)
    return factor_of


def normal_values(rng, dims, deviation, limit, pieces=(), kind=jnp.bfloat16):
    factor_of = block_levels(rng, dims, pieces, -0.22, 0.18) if pieces else 1.0
    values = jax.random.normal(rng, dims, jnp.float32) * deviation * factor_of
    return jnp.minimum(jnp.maximum(values, -limit), limit).astype(kind)


def noise_with(key, dims, scale, bound, cuts, heavy, kind=jnp.bfloat16):
    entries = scale * jax.random.normal(key, dims, jnp.float32)
    if cuts:
        entries = entries * block_levels(key, dims, cuts, -0.22, 0.18)
    return jnp.clip(raised(entries, jax.random.fold_in(key, 3), *heavy), -bound, bound).astype(kind)


def setup_inputs(seed: int = 0) -> dict:
    splits = jax.random.split(jax.random.key(seed), 15)
    tokens = normal_values(splits[0], (N_DP * MICRO, ROWS, D), 1.0, 6.0, ((0, 8),))
    group_ids = draw_group_ids(jax.random.fold_in(splits[14], 71), 0)
    type_ids = draw_type_ids(jax.random.fold_in(splits[14], 71), 0)
    norm_gain = jnp.clip(1.0 + 0.1 * jax.random.normal(splits[3], (SECTIONS, D), jnp.float32), 0.5, 1.5).astype(jnp.bfloat16)
    norm_bias = normal_values(splits[4], (SECTIONS, D), 0.3, 1.75, ((0, 4),))
    qkv_weight = normal_values(splits[5], (LAYERS, D, 3 * D), D ** -0.5, 0.21875)
    qv_bias = normal_values(splits[6], (LAYERS, 2, D), 0.3, 1.75)
    out_weight = normal_values(splits[7], (LAYERS, D, D), (D // 64) ** -0.5, 1.75)
    out_bias = normal_values(splits[8], (LAYERS, D), 0.3, 1.75)
    up_weight = normal_values(splits[9], (3, D, FF), D ** -0.5, 0.21875)
    up_bias = normal_values(splits[10], (3, FF), 0.3, 1.75)
    down_weight = normal_values(splits[11], (3, FF, D), FF ** -0.5, 0.109375)
    down_bias = normal_values(splits[12], (3, D), 0.3, 1.75)
    out_cotangent = noise_with(splits[13], (N_DP * MICRO, ROWS, D), 1.0, 8.0, ((0, 8),), (0, 2, 8, 2.0))
    return dict(tokens=tokens, group_ids=group_ids, type_ids=type_ids, norm_gain=norm_gain, norm_bias=norm_bias, qkv_weight=qkv_weight, qv_bias=qv_bias, out_weight=out_weight, out_bias=out_bias, up_weight=up_weight, up_bias=up_bias, down_weight=down_weight, down_bias=down_bias, out_cotangent=out_cotangent)


@jax.custom_vjp
def low(v):
    return lax.optimization_barrier(v.astype(jnp.bfloat16)).astype(jnp.float32)

@jax.custom_vjp
def low_back(v):
    return v

def low_keep(v):
    return (low(v), None)

def low_pass(kept, grad):
    return (grad,)

def back_keep(v):
    return (v, None)

def back_low(kept, grad):
    return (low(grad),)
low.defvjp(low_keep, low_pass)
low_back.defvjp(back_keep, back_low)

def normalize(values, scale_row, shift_row):
    center = values - lax.optimization_barrier(jnp.mean(values, axis=-1, keepdims=True))
    spread = lax.optimization_barrier(jnp.mean(center * center, axis=-1, keepdims=True))
    return center * lax.rsqrt(spread + 1e-05) * scale_row + shift_row

def smooth_gelu(values):
    return 0.5 * values * (1.0 + jnp.tanh(0.7978845608028654 * (values + 0.044715 * values * values * values)))

def attention_section(hidden, same_group, weight_set):
    scale_row, shift_row, qkv_proj, qv_shift, out_proj, out_shift = weight_set
    highest = lax.Precision.HIGHEST
    row_count = hidden.shape[0]
    attn_in = low(normalize(hidden, scale_row, shift_row))
    zero_bias = jnp.zeros_like(qv_shift[0])
    bias_row = jnp.concatenate([qv_shift[0], zero_bias, qv_shift[1]])
    projected = low_back(low(jnp.dot(attn_in, qkv_proj, precision=highest) + bias_row))
    queries = projected[:, :D].reshape(row_count, H, HD)
    keys_part = projected[:, D:2 * D].reshape(row_count, H, HD)
    values_part = projected[:, 2 * D:].reshape(row_count, H, HD)
    scores = low_back(jnp.einsum('qhd,khd->hqk', queries, keys_part, precision=highest) * HD ** (-0.5))
    scores = jnp.where(same_group[None], scores, -1e+30)
    shifted = scores - lax.optimization_barrier(jnp.max(scores, axis=-1, keepdims=True))
    exponent = jnp.exp(shifted)
    attention = exponent / lax.optimization_barrier(jnp.sum(exponent, axis=-1, keepdims=True))
    context = jnp.einsum('hqk,khd->qhd', low(attention), values_part, precision=highest).reshape(row_count, D)
    context = low_back(low(context))
    return low_back(low(hidden + (jnp.dot(context, out_proj, precision=highest) + out_shift)))

def expert_section(hidden, is_image, weight_set):
    scale_row, shift_row, up_proj, up_shift, down_proj, down_shift = weight_set
    highest = lax.Precision.HIGHEST
    ffn_in = low(normalize(hidden, scale_row, shift_row))
    pre_act = low_back(jnp.einsum('rd,edf->ref', ffn_in, up_proj, precision=highest) + up_shift)
    activated = low(smooth_gelu(pre_act))
    expert_out = jnp.einsum('ref,efd->red', activated, down_proj, precision=highest) + down_shift
    if up_proj.shape[0] == 2:
        chosen = jnp.where(is_image[:, None], expert_out[:, 0], expert_out[:, 1])
    else:
        chosen = expert_out[:, 0]
    return low_back(low(hidden + chosen))

def reference(tokens, group_ids, type_ids, norm_gain, norm_bias, qkv_weight, qv_bias, out_weight, out_bias, up_weight, up_bias, down_weight, down_bias, out_cotangent):
    weights = tuple((member.astype(jnp.float32) for member in (norm_gain, norm_bias, qkv_weight, qv_bias, out_weight, out_bias, up_weight, up_bias, down_weight, down_bias)))
    same_group = group_ids[:, :, None] == group_ids[:, None, :]
    is_image = type_ids == 0

    def run_stack(weight_set, inputs):
        scale_all, shift_all, qkv_all, qv_all, out_all, out_shift_all, up_all, up_shift_all, down_all, down_shift_all = weight_set

        def one_row(operands):
            hidden, same_row, image_row = operands
            hidden = attention_section(hidden, same_row, (scale_all[0], shift_all[0], qkv_all[0], qv_all[0], out_all[0], out_shift_all[0]))
            hidden = expert_section(hidden, image_row, (scale_all[1], shift_all[1], up_all[0:2], up_shift_all[0:2], down_all[0:2], down_shift_all[0:2]))
            hidden = attention_section(hidden, same_row, (scale_all[2], shift_all[2], qkv_all[1], qv_all[1], out_all[1], out_shift_all[1]))
            hidden = expert_section(hidden, image_row, (scale_all[3], shift_all[3], up_all[2:3], up_shift_all[2:3], down_all[2:3], down_shift_all[2:3]))
            return hidden
        return lax.map(jax.checkpoint(one_row), (inputs, same_group, is_image))
    outputs, pullback = jax.vjp(run_stack, weights, tokens.astype(jnp.float32))
    weight_grads, input_grad = pullback(out_cotangent.astype(jnp.float32))
    scale_grad, shift_grad, qkv_grad, qv_grad, proj_grad, proj_shift_grad, up_grad, up_shift_grad, down_grad, down_shift_grad = weight_grads
    return (outputs.astype(jnp.bfloat16), input_grad, scale_grad, shift_grad, qkv_grad, qv_grad, proj_grad, proj_shift_grad, up_grad, up_shift_grad, down_grad, down_shift_grad)
```

```python
from functools import partial
import math

import jax
import jax.numpy as jnp
from jax import lax
from jax.experimental import pallas as pl
from jax.experimental.pallas import tpu as pltpu
from jax.sharding import PartitionSpec as P

D = 768
H = 12
HD = 64
FF = 3072
PATCHES = 197


def shortened(value):

    def short(part):
        return part.astype(jnp.bfloat16) if part.dtype == jnp.float32 else part

    return jax.tree.map(short, value)


def shifted_2(value, axis, steps):
    count = lax.axis_size(axis)
    leading, last = (max(0, -steps), min(count, count - steps))
    return lax.ppermute(value, axis, [(source, source + steps) for source in range(leading, last)])


def spread_2(value, axis, root):
    mine = lax.axis_index(axis) == root
    return lax.psum(jnp.where(mine, value, jnp.zeros_like(value)), axis)


def normalize(values, scale_row, shift_row):
    center = values - jnp.mean(values, axis=-1, keepdims=True)
    spread = jnp.mean(center * center, axis=-1, keepdims=True)
    return center * lax.rsqrt(spread + 1e-05) * scale_row + shift_row


def smooth_gelu(values):
    return (
        0.5
        * values
        * (1.0 + jnp.tanh(0.7978845608028654 * (values + 0.044715 * values * values * values)))
    )


def text_rows(image_start, row_count):
    text_spots = jnp.arange(row_count - PATCHES, dtype=jnp.int32)
    return text_spots + jnp.where(text_spots >= image_start, PATCHES, 0).astype(jnp.int32)


def split_routes(values, image_start, text_index):
    return (
        lax.dynamic_slice_in_dim(values, image_start, PATCHES, 0),
        jnp.take(values, text_index, axis=0),
    )


def place_rows(image_part, text_part, image_start, text_index):
    merged = jnp.zeros(
        (image_part.shape[0] + text_part.shape[0], image_part.shape[1]), image_part.dtype
    )
    merged = merged.at[text_index].set(text_part)
    return lax.dynamic_update_slice_in_dim(merged, image_part, image_start, 0)


def attention_forward(hidden, same_group, scale_row, shift_row, weight_set):
    qkv_proj, qv_shift, out_proj, out_shift = weight_set
    row_count = hidden.shape[0]
    attn_in = normalize(hidden, scale_row, shift_row).astype(jnp.bfloat16)
    zero_bias = jnp.zeros((D,), jnp.float32)
    bias_row = jnp.concatenate(
        [qv_shift[0].astype(jnp.float32), zero_bias, qv_shift[1].astype(jnp.float32)]
    )
    projected = (jnp.dot(attn_in, qkv_proj, preferred_element_type=jnp.float32) + bias_row).astype(
        jnp.bfloat16
    )
    queries = projected[:, :D].reshape(row_count, H, HD)
    keys_part = projected[:, D : 2 * D].reshape(row_count, H, HD)
    values_part = projected[:, 2 * D :].reshape(row_count, H, HD)
    scores = jnp.einsum(
        "qhd,khd->hqk", queries, keys_part, preferred_element_type=jnp.float32
    ) * HD ** (-0.5)
    scores = jnp.where(same_group[None], scores, -1e30)
    shifted = scores - jnp.max(scores, axis=-1, keepdims=True)
    exponent = jnp.exp(shifted)
    attention = exponent / jnp.sum(exponent, axis=-1, keepdims=True)
    attention_low = attention.astype(jnp.bfloat16)
    context = jnp.einsum(
        "hqk,khd->qhd", attention_low, values_part, preferred_element_type=jnp.float32
    )
    context = context.reshape(row_count, D).astype(jnp.bfloat16)
    result_block = hidden + (
        jnp.dot(context, out_proj, preferred_element_type=jnp.float32)
        + out_shift.astype(jnp.float32)
    )
    return (
        result_block,
        (attn_in, queries, keys_part, values_part, attention, attention_low, context),
    )


def attention_backward(grad_low, hidden, same_group, scale_row, shift_row, weight_set):
    qkv_proj, qv_shift, out_proj, out_shift = weight_set
    _, kept_values = attention_forward(hidden, same_group, scale_row, shift_row, weight_set)
    attn_in, queries, keys_part, values_part, attention, attention_low, context = kept_values
    row_count = hidden.shape[0]
    grad_out = grad_low.astype(jnp.float32)
    out_proj_grad = jnp.einsum("rd,re->de", context, grad_low, preferred_element_type=jnp.float32)
    out_shift_grad = jnp.sum(grad_out, axis=0)
    context_grad = jnp.einsum("re,de->rd", grad_low, out_proj, preferred_element_type=jnp.float32)
    context_grad = context_grad.astype(jnp.bfloat16).reshape(row_count, H, HD)
    values_grad = jnp.einsum(
        "hqk,qhd->khd", attention_low, context_grad, preferred_element_type=jnp.float32
    )
    attention_grad = jnp.einsum(
        "qhd,khd->hqk", context_grad, values_part, preferred_element_type=jnp.float32
    )
    scores_grad = attention * (
        attention_grad - jnp.sum(attention_grad * attention, axis=-1, keepdims=True)
    )
    scores_grad = scores_grad.astype(jnp.bfloat16)
    queries_grad = jnp.einsum(
        "hqk,khd->qhd", scores_grad, keys_part, preferred_element_type=jnp.float32
    ) * HD ** (-0.5)
    keys_grad = jnp.einsum(
        "hqk,qhd->khd", scores_grad, queries, preferred_element_type=jnp.float32
    ) * HD ** (-0.5)
    projected_grad = jnp.concatenate(
        [
            queries_grad.reshape(row_count, D),
            keys_grad.reshape(row_count, D),
            values_grad.reshape(row_count, D),
        ],
        axis=1,
    ).astype(jnp.bfloat16)
    qv_shift_grad = jnp.stack(
        [
            jnp.sum(projected_grad[:, :D].astype(jnp.float32), axis=0),
            jnp.sum(projected_grad[:, 2 * D :].astype(jnp.float32), axis=0),
        ]
    )
    qkv_proj_grad = jnp.einsum(
        "rd,re->de", attn_in, projected_grad, preferred_element_type=jnp.float32
    )
    attn_in_grad = jnp.einsum(
        "re,de->rd", projected_grad, qkv_proj, preferred_element_type=jnp.float32
    )
    hidden_part, scale_grad, shift_grad = jax.vjp(normalize, hidden, scale_row, shift_row)[1](
        attn_in_grad
    )
    return (
        grad_out + hidden_part,
        [scale_grad, shift_grad, qkv_proj_grad, qv_shift_grad, out_proj_grad, out_shift_grad],
    )


def expert_inputs(ffn_in, image_start, routed):
    row_count = ffn_in.shape[0]
    text_index = text_rows(image_start, row_count)
    if not routed:
        return ((ffn_in,), text_index)
    return (split_routes(ffn_in, image_start, text_index), text_index)


def expert_forward(hidden, image_start, scale_row, shift_row, weight_set):
    up_proj, up_shift, down_proj, down_shift, routed = weight_set
    ffn_in = normalize(hidden, scale_row, shift_row).astype(jnp.bfloat16)
    inputs, text_index = expert_inputs(ffn_in, image_start, routed)
    pre_acts = tuple(
        (
            jnp.dot(inputs[expert], up_proj[expert], preferred_element_type=jnp.float32)
            + up_shift[expert].astype(jnp.float32)
            for expert in range(len(inputs))
        )
    )
    activated = tuple((smooth_gelu(pre_act).astype(jnp.bfloat16) for pre_act in pre_acts))
    expert_outs = tuple(
        (
            jnp.dot(activated[expert], down_proj[expert], preferred_element_type=jnp.float32)
            + down_shift[expert].astype(jnp.float32)
            for expert in range(len(inputs))
        )
    )
    if not routed:
        joined = expert_outs[0]
    else:
        joined = place_rows(expert_outs[0], expert_outs[1], image_start, text_index)
    return (hidden + joined, (inputs, pre_acts, activated, text_index))


def expert_backward(grad_low, hidden, image_start, scale_row, shift_row, weight_set):
    up_proj, up_shift, down_proj, down_shift, routed = weight_set
    _, kept_values = expert_forward(hidden, image_start, scale_row, shift_row, weight_set)
    inputs, pre_acts, activated, text_index = kept_values
    grad_out = grad_low.astype(jnp.float32)
    if not routed:
        grad_parts = (grad_low,)
    else:
        grad_parts = split_routes(grad_low, image_start, text_index)
    up_grads, up_shift_grads, down_grads, down_shift_grads, input_grads = ([], [], [], [], [])
    for expert in range(len(inputs)):
        expert_grad = grad_parts[expert]
        down_grads.append(
            jnp.einsum(
                "rf,rd->fd", activated[expert], expert_grad, preferred_element_type=jnp.float32
            )
        )
        down_shift_grads.append(jnp.sum(expert_grad.astype(jnp.float32), axis=0))
        act_grad = jnp.einsum(
            "rd,fd->rf", expert_grad, down_proj[expert], preferred_element_type=jnp.float32
        )
        pre_grad = jax.vjp(smooth_gelu, pre_acts[expert])[1](act_grad)[0].astype(jnp.bfloat16)
        up_grads.append(
            jnp.einsum("rd,rf->df", inputs[expert], pre_grad, preferred_element_type=jnp.float32)
        )
        up_shift_grads.append(jnp.sum(pre_grad.astype(jnp.float32), axis=0))
        input_grads.append(
            jnp.einsum("rf,df->rd", pre_grad, up_proj[expert], preferred_element_type=jnp.float32)
        )
    if not routed:
        ffn_in_grad = input_grads[0]
    else:
        ffn_in_grad = place_rows(input_grads[0], input_grads[1], image_start, text_index)
    hidden_part, scale_grad, shift_grad = jax.vjp(normalize, hidden, scale_row, shift_row)[1](
        ffn_in_grad
    )
    return (
        grad_out + hidden_part,
        [
            scale_grad,
            shift_grad,
            jnp.stack(up_grads),
            jnp.stack(up_shift_grads),
            jnp.stack(down_grads),
            jnp.stack(down_shift_grads),
        ],
    )


def attention_layout():
    return [((D,), 0), ((D,), 0), ((D, 3 * D), 0), ((2, D), 1), ((D, D), 0), ((D,), 0)]


def expert_layout(experts_here):
    return [
        ((D,), 0),
        ((D,), 0),
        ((experts_here, D, FF), 1),
        ((experts_here, FF), 1),
        ((experts_here, FF, D), 1),
        ((experts_here, D), 1),
    ]


def section_layouts():
    return [attention_layout(), expert_layout(2), attention_layout(), expert_layout(1)]


def layout_entries(layout):
    return sum((math.prod(full_shape) for full_shape, split_dim in layout))


def padded_width(entries):
    return -(-entries // 128) * 128


def split_rows(grad_term, split_dim, group_count):
    full_shape = grad_term.shape
    pieces_all = grad_term.reshape(
        full_shape[:split_dim]
        + (group_count, full_shape[split_dim] // group_count)
        + full_shape[split_dim + 1 :]
    )
    return jnp.moveaxis(pieces_all, split_dim, 0).reshape(group_count, -1)


def fit_width(flat_terms, width):
    return jnp.pad(flat_terms, ((0, 0), (0, width - flat_terms.shape[1])))


def pack_terms(grad_terms, layout, group_count, pack_width):
    flat_terms = jnp.concatenate(
        [
            split_rows(grad_term, split_dim, group_count)
            for grad_term, (full_shape, split_dim) in zip(grad_terms, layout)
        ],
        axis=1,
    )
    return fit_width(flat_terms, pack_width)


def unpack_row(flat_row, layout, group_count):
    results = []
    offset = 0
    for full_shape, split_dim in layout:
        shard_shape = (
            full_shape[:split_dim]
            + (full_shape[split_dim] // group_count,)
            + full_shape[split_dim + 1 :]
        )
        entries = math.prod(shard_shape)
        results.append(flat_row[offset : offset + entries].reshape(shard_shape))
        offset = offset + entries
    return results


def per_device(
    tokens,
    group_ids,
    type_ids,
    norm_gain,
    norm_bias,
    qkv_weight,
    qv_bias,
    out_weight,
    out_bias,
    up_weight,
    up_bias,
    down_weight,
    down_bias,
    out_cotangent,
):
    segment_count = lax.axis_size("segment")
    segment_place = lax.axis_index("segment")
    group_count = lax.axis_size("dp")
    micro_count = tokens.shape[0]
    row_count = tokens.shape[1]
    tick_count = micro_count + segment_count - 1
    scale_row = norm_gain[0].astype(jnp.float32)
    shift_row = norm_bias[0].astype(jnp.float32)
    layouts = section_layouts()
    pack_width = padded_width(max((layout_entries(layout) for layout in layouts)) // group_count)
    same_all = group_ids[:, :, None] == group_ids[:, None, :]
    row_spots = jnp.arange(row_count, dtype=jnp.int32)[None, :]
    image_starts = jnp.min(jnp.where(type_ids == 0, row_spots, row_count), axis=1)
    attention_sets = tuple(
        (
            (
                qkv_weight[layer_index],
                qv_bias[layer_index],
                out_weight[layer_index],
                out_bias[layer_index],
            )
            for layer_index in range(2)
        )
    )
    expert_sets = (
        (up_weight[0:2], up_bias[0:2], down_weight[0:2], down_bias[0:2], True),
        (up_weight[2:3], up_bias[2:3], down_weight[2:3], down_bias[2:3], False),
    )

    def forward_branch(section, block_in, position):
        if section % 2 == 0:
            result_block = attention_forward(
                block_in, same_all[position], scale_row, shift_row, attention_sets[section // 2]
            )[0]
        else:
            result_block = expert_forward(
                block_in, image_starts[position], scale_row, shift_row, expert_sets[section // 2]
            )[0]
        return result_block.astype(jnp.bfloat16)

    def forward_tick(tick_index, loop_state):
        incoming, kept_inputs, finals = loop_state
        micro_index = tick_index - segment_place
        active = (micro_index >= 0) & (micro_index < micro_count)
        position = jnp.clip(micro_index, 0, micro_count - 1)
        given_block = jnp.where(segment_place == 0, tokens[position], incoming)

        def forward_compute(block_in):
            return lax.switch(
                segment_place,
                [partial(forward_branch, section) for section in range(segment_count)],
                block_in.astype(jnp.float32),
                position,
            )

        def forward_resting(block_in):
            return jnp.zeros_like(block_in)

        result_block = lax.cond(active, forward_compute, forward_resting, given_block)
        kept_inputs = kept_inputs.at[position].set(
            jnp.where(active, given_block, kept_inputs[position])
        )
        finals = finals.at[position].set(jnp.where(active, result_block, finals[position]))
        incoming = jax.tree.map(
            lambda part, own: part.astype(own.dtype),
            shifted_2(shortened(result_block), "segment", 1),
            result_block,
        )
        return (incoming, kept_inputs, finals)

    zero_block = jnp.zeros(tokens.shape[1:], jnp.bfloat16)
    stash_zero = jnp.zeros(tokens.shape, jnp.bfloat16)
    _, kept_inputs, finals = lax.fori_loop(
        0, tick_count, forward_tick, (zero_block, stash_zero, stash_zero)
    )

    def backward_branch(section, grad_low, position):
        hidden = kept_inputs[position].astype(jnp.float32)
        if section % 2 == 0:
            hidden_grad, grad_terms = attention_backward(
                grad_low,
                hidden,
                same_all[position],
                scale_row,
                shift_row,
                attention_sets[section // 2],
            )
        else:
            hidden_grad, grad_terms = expert_backward(
                grad_low,
                hidden,
                image_starts[position],
                scale_row,
                shift_row,
                expert_sets[section // 2],
            )
        return (hidden_grad, pack_terms(grad_terms, layouts[section], group_count, pack_width))

    def backward_tick(tick_index, loop_state):
        incoming, input_grads, totals = loop_state
        micro_index = tick_index - (segment_count - 1 - segment_place)
        active = (micro_index >= 0) & (micro_index < micro_count)
        position = jnp.clip(micro_index, 0, micro_count - 1)
        given_block = jnp.where(
            segment_place == segment_count - 1, out_cotangent[position], incoming
        )

        def backward_compute(block_in):
            return lax.switch(
                segment_place,
                [partial(backward_branch, section) for section in range(segment_count)],
                block_in,
                position,
            )

        def backward_resting(block_in):
            return (
                jnp.zeros(block_in.shape, jnp.float32),
                jnp.zeros((group_count, pack_width), jnp.float32),
            )

        hidden_grad, flat_terms = lax.cond(active, backward_compute, backward_resting, given_block)
        input_grads = input_grads.at[position].set(
            jnp.where(active, hidden_grad, input_grads[position])
        )
        totals = totals + flat_terms
        incoming = shifted_2(hidden_grad.astype(jnp.bfloat16), "segment", -1)
        return (incoming, input_grads, totals)

    grads_zero = jnp.zeros(tokens.shape, jnp.float32)
    totals_start = jnp.zeros((group_count, pack_width), jnp.float32)
    _, input_grads, totals = lax.fori_loop(
        0, tick_count, backward_tick, (zero_block, grads_zero, totals_start)
    )
    width_d = D // group_count
    shares = lax.psum_scatter(totals, "dp", scatter_dimension=0, tiled=True)
    gathered = lax.all_gather(shares.astype(jnp.bfloat16), "segment", axis=0, tiled=True).astype(
        shares.dtype
    )
    norm_gain_grad = shares[0, :width_d].reshape(1, width_d)
    norm_bias_grad = shares[0, width_d : 2 * width_d].reshape(1, width_d)
    first_attention = unpack_row(gathered[0], layouts[0], group_count)
    both_experts = unpack_row(gathered[1], layouts[1], group_count)
    second_attention = unpack_row(gathered[2], layouts[2], group_count)
    uniting_expert = unpack_row(gathered[3], layouts[3], group_count)
    qkv_weight_grad = jnp.stack([first_attention[2], second_attention[2]])
    qv_bias_grad = jnp.stack([first_attention[3], second_attention[3]])
    out_weight_grad = jnp.stack([first_attention[4], second_attention[4]])
    out_bias_grad = jnp.stack([first_attention[5], second_attention[5]])
    up_weight_grad = jnp.concatenate([both_experts[2], uniting_expert[2]], axis=0)
    up_bias_grad = jnp.concatenate([both_experts[3], uniting_expert[3]], axis=0)
    down_weight_grad = jnp.concatenate([both_experts[4], uniting_expert[4]], axis=0)
    down_bias_grad = jnp.concatenate([both_experts[5], uniting_expert[5]], axis=0)
    own_rows = row_count // segment_count
    final_all = spread_2(finals, "segment", segment_count - 1)
    input_all = spread_2(input_grads.astype(jnp.bfloat16), "segment", 0).astype(input_grads.dtype)
    layer_output = lax.dynamic_slice_in_dim(final_all, segment_place * own_rows, own_rows, 1)
    input_grad = lax.dynamic_slice_in_dim(input_all, segment_place * own_rows, own_rows, 1)
    return (
        layer_output,
        input_grad,
        norm_gain_grad,
        norm_bias_grad,
        qkv_weight_grad,
        qv_bias_grad,
        out_weight_grad,
        out_bias_grad,
        up_weight_grad,
        up_bias_grad,
        down_weight_grad,
        down_bias_grad,
    )


F32 = jnp.float32
BF16 = jnp.bfloat16
MESH = pl.DeviceIdType.MESH
MIB = 2**20


def mm(a, b):
    return lax.dot_general(a, b, (((1,), (0,)), ((), ())), preferred_element_type=F32)


def mm_t(a, b):
    return lax.dot_general(a, b, (((1,), (1,)), ((), ())), preferred_element_type=F32)


def ln_parts(h):
    center = h - jnp.mean(h, axis=-1, keepdims=True)
    r = lax.rsqrt(jnp.mean(center * center, axis=-1, keepdims=True) + 1e-05)
    return center * r, r


def gelu_both(x):
    x2 = x * x
    t = jnp.tanh(0.7978845608028654 * (x + 0.044715 * x2 * x))
    half = 0.5 * (1.0 + t)
    slope = half + (0.5 * x) * (1.0 - t * t) * (
        0.7978845608028654 + (3.0 * 0.044715 * 0.7978845608028654) * x2
    )
    return x * half, slope


def places():
    seg = lax.axis_index("segment")
    dp = lax.axis_index("dp")
    return seg, dp, dp // 2, dp % 2, seg // 2, seg % 2


def chain_kernel(
    tok, cot, oh, gb, sm, ub, wq_h, wo_h, wu_h, wd_h,
    x1o, x3o, g2o, c4o, pao, comb, smo,
    wq, wo, wu, wd, hbuf, xa, proj, kvo, ctx, prob, bias, xf1, xf3, act, acts, dg1, dg1s, dg3,
    gbuf, cg, pga, dks, dkr, lt, pb, dxs, full, pieces, gball, ohv,
    w_sem, in_sem, gs_sem, gr_sem, ts_sem, tr_sem, c_sem, cs_sem, cr_sem, kvs_sem, kvr_sem,
    dks_sem, dkr_sem, as_sem, ar_sem, al_sem, pb_sem, fs_sem, fr_sem, us_sem, ur_sem, g4_sem,
):
    seg, dp, z, k, y, x = places()
    other = 1 - k
    partner = (seg, 2 * z + other)

    def peer(d):
        return ((seg + d) % 4, dp)

    def back(d):
        return (seg + 4 - d) % 4

    loads = {}

    def load(name, src, dst, sem):
        copy = pltpu.make_async_copy(src, dst, sem)
        copy.start()
        loads[name] = copy

    load("q0", wq_h.at[0], wq.at[0], w_sem.at[0])
    load("o0", wo_h.at[0], wo.at[0], w_sem.at[1])

    barrier = pltpu.get_barrier_semaphore()
    for d in range(4):
        for c in range(2):
            if d == 0 and c == 1:
                continue
            where = partner if d == 0 else ((seg + d) % 4, 2 * z + c)
            pl.semaphore_signal(barrier, inc=1, device_id=where, device_id_type=MESH)
    pl.semaphore_wait(barrier, 7)

    def remote(src, dst, ssem, rsem, where):
        return pltpu.make_async_remote_copy(
            src_ref=src, dst_ref=dst, send_sem=ssem, recv_sem=rsem,
            device_id=where, device_id_type=MESH,
        )

    own_tok = pl.ds(pl.multiple_of(256 * k, 256), 256)
    far_tok = pl.ds(pl.multiple_of(256 * other, 256), 256)
    tok_here = pltpu.make_async_copy(tok.at[x, own_tok], hbuf.at[0], in_sem.at[0])
    oh_here = pltpu.make_async_copy(oh.at[x], ohv, in_sem.at[1])
    tok_far = remote(tok.at[x, far_tok], hbuf.at[0], ts_sem.at[0], tr_sem.at[0], partner)
    oh_far = remote(oh.at[x], ohv, ts_sem.at[1], tr_sem.at[1], partner)

    @pl.when(k == y)
    def _():
        tok_here.start()
        oh_here.start()
        tok_far.start()
        oh_far.start()

    gains = [
        remote(gb, gball.at[seg], gs_sem.at[d - 1], gr_sem.at[d - 1], peer(d)) for d in (1, 2, 3)
    ]
    for copy in gains:
        copy.start()
    load("u0", wu_h.at[0], wu.at[0], w_sem.at[2])
    load("u1", wu_h.at[1], wu.at[1], w_sem.at[3])
    load("d0", wd_h.at[0], wd.at[0], w_sem.at[4])
    load("d1", wd_h.at[1], wd.at[1], w_sem.at[5])
    cots = []
    for m in range(2):
        here = pltpu.make_async_copy(cot.at[m, own_tok], c4o.at[2 * k + m], c_sem.at[m])
        there = remote(
            cot.at[m, far_tok], c4o.at[2 * k + m], cs_sem.at[m], cr_sem.at[m], partner
        )
        here.start()
        there.start()
        cots.append((here, there))
    load("q1", wq_h.at[1], wq.at[1], w_sem.at[6])
    load("o1", wo_h.at[1], wo.at[1], w_sem.at[7])

    gball[seg] = gb[...]
    smo[...] = jnp.zeros_like(smo)
    for copy in gains:
        copy.wait()

    @pl.when(k == y)
    def _():
        tok_here.wait()
        oh_here.wait()
        tok_far.wait_send()
        oh_far.wait_send()

    @pl.when(k != y)
    def _():
        tok_far.wait_recv()
        oh_far.wait_recv()

    group_lane = (lax.broadcasted_iota(jnp.int32, (256, 128), 1) < 3).astype(F32).astype(BF16)
    mine = ohv[own_tok, :] * group_lane
    theirs = ohv[far_tok, :]
    same = mm_t(jnp.concatenate([ohv[own_tok, :], theirs], axis=0), mine)
    bias[...] = jnp.where(same > 0.5, 0.0, -1e30)

    lane = lax.broadcasted_iota(jnp.int32, (1, 128), 1)
    head_mask = [(lane < 64).astype(F32).astype(BF16), (lane >= 64).astype(F32).astype(BF16)]
    head_scaled = [part * 0.125 for part in head_mask]

    def gain_of(s):
        return gball[s, 0:1, :], gball[s, 1:2, :]

    def normed(s):
        n, _ = ln_parts(hbuf[s].astype(F32))
        gain, shift = gain_of(s)
        return (n * gain + shift).astype(BF16)

    def lanes(start, width):
        return pl.ds(pl.multiple_of(start, 128), width)

    def attn_fwd(l):
        s = 2 * l
        xin = normed(s)
        xa[l] = xin
        loads[f"q{l}"].wait()
        kv = remote(
            proj.at[l, :, pl.ds(768, 1536)], kvo.at[l], kvs_sem.at[l], kvr_sem.at[l], partner
        )
        for n in (1, 2, 0):
            part = mm(xin, wq[l, :, 768 * n : 768 * (n + 1)])
            if n != 1:
                row = 2 * l + (n == 2)
                part = part + sm[row : row + 1, :]
            proj[l, :, 768 * n : 768 * (n + 1)] = part.astype(BF16)
            if n == 2:
                kv.start()
        kv.wait()

        def pair(hp, carry):
            lo = hp * 128
            q = proj[l, :, lanes(lo, 128)]
            kk = jnp.concatenate([proj[l, :, lanes(768 + lo, 128)], kvo[l, :, lanes(lo, 128)]], 0)
            vv = jnp.concatenate(
                [proj[l, :, lanes(1536 + lo, 128)], kvo[l, :, lanes(768 + lo, 128)]], 0
            )
            vt = vv.T
            outs = []
            for j in range(2):
                st = mm_t(kk, q * head_scaled[j]) + bias[...]
                e = jnp.exp(st - jnp.max(st, axis=0, keepdims=True))
                p = (e * (1.0 / jnp.sum(e, axis=0, keepdims=True))).astype(BF16)
                prob[l, 2 * hp + j] = p
                outs.append(mm(vt[64 * j : 64 * (j + 1)], p))
            ctx[l, :, lanes(lo, 128)] = jnp.concatenate(outs, 0).T.astype(BF16)
            return carry

        lax.fori_loop(0, 6, pair, 0)
        loads[f"o{l}"].wait()
        out = mm(ctx[l], wo[l]) + sm[4 + l : 5 + l, :]
        hbuf[s + 1] = (hbuf[s].astype(F32) + out).astype(BF16)

    def ffn_up(rows_in, slot, e, act_ref, dg_ref):
        def step(n, carry):
            at = lanes(256 * n, 256)
            pre = mm(rows_in, wu[slot, :, at]) + ub[12 * e + n]
            a, slope = gelu_both(pre)
            act_ref[:, at] = a.astype(BF16)
            dg_ref[:, at] = slope.astype(BF16)
            return carry

        lax.fori_loop(0, 12, step, 0)

    def ffn_down(act_ref, slot, e):
        return mm(act_ref[...], wd[slot]) + sm[pl.ds(8 + e, 1), :]

    row = lax.broadcasted_iota(jnp.int32, (256, 1), 0)
    is_first = ((row < PATCHES) | (k == 1)).astype(F32)
    is_second = ((row >= PATCHES) & (k == 0)).astype(F32)

    def push_all(src, dst, slot):
        local = pltpu.make_async_copy(src, dst.at[seg], al_sem.at[slot])
        local.start()
        copies = [
            remote(src, dst.at[seg], as_sem.at[slot, d - 1], ar_sem.at[slot, d - 1], peer(d))
            for d in (1, 2, 3)
        ]
        for copy in copies:
            copy.start()
        return local, copies

    attn_fwd(0)

    xf1[...] = normed(1)
    sent1 = push_all(xf1, x1o, 0)
    loads["u0"].wait()
    loads["u1"].wait()
    ffn_up(xf1[...], k, k, act, dg1)
    ffn_up(xf1[192:256, :], 1, 1, acts, dg1s)
    loads["d0"].wait()
    loads["d1"].wait()
    dxs[...] = ffn_down(act, k, k)
    second = ffn_down(acts, 1, 1)
    m2 = is_second[192:256]
    dxs[192:256, :] = jnp.where(m2 > 0.5, second, dxs[192:256, :])
    hbuf[2] = (hbuf[1].astype(F32) + dxs[...]).astype(BF16)
    load("u2", wu_h.at[2], wu.at[0], w_sem.at[8])
    load("d2", wd_h.at[2], wd.at[0], w_sem.at[9])

    attn_fwd(1)

    xf3[...] = normed(3)
    sent3 = push_all(xf3, x3o, 1)
    loads["u2"].wait()
    ffn_up(xf3[...], 0, 2, act, dg3)
    loads["d2"].wait()
    for m in range(2):
        cots[m][0].wait()
        cots[m][1].wait()
    g4 = pltpu.make_async_copy(c4o.at[seg], gbuf.at[3], g4_sem)
    g4.start()
    h4 = (hbuf[3].astype(F32) + ffn_down(act, 0, 2)).astype(BF16)
    hbuf[4] = h4
    g4.wait()

    def ffn_back(g, slot, e, act_ref, dg_ref):
        def step(n, carry):
            at = lanes(256 * n, 256)
            ag = mm_t(g, wd[slot, pl.ds(pl.multiple_of(256 * n, 256), 256), :])
            pg = (ag * dg_ref[:, at].astype(F32)).astype(BF16)
            act_ref[:, at] = pg
            spot = (pl.ds(14 + 4 * e + n // 3, 1), lanes(256 * (n % 3), 256))
            smo[spot] = smo[spot] + jnp.sum(pg.astype(F32), axis=0, keepdims=True)
            return carry

        lax.fori_loop(0, 12, step, 0)
        return mm_t(act_ref[...], wu[slot])

    def norm_back(s, g):
        n, r = ln_parts(hbuf[s].astype(F32))
        gain, _ = gain_of(s)
        dx = dxs[...]
        smo[s : s + 1, :] = jnp.sum(dx * n, axis=0, keepdims=True)
        smo[4 + s : 5 + s, :] = jnp.sum(dx, axis=0, keepdims=True)
        c = dx * gain
        return g.astype(F32) + r * (
            c - jnp.mean(c, axis=-1, keepdims=True) - n * jnp.mean(c * n, axis=-1, keepdims=True)
        )

    g = gbuf[3]
    smo[28:29, :] = jnp.sum(g.astype(F32), axis=0, keepdims=True)
    dxs[...] = ffn_back(g, 0, 2, act, dg3)
    load("u3", wu_h.at[0], wu.at[0], w_sem.at[2])
    load("d3", wd_h.at[0], wd.at[0], w_sem.at[4])
    gbuf[2] = norm_back(3, g).astype(BF16)

    pb_copies = []

    def attn_back(l):
        s = 2 * l
        g = gbuf[s]
        smo[12 + l : 13 + l, :] = jnp.sum(g.astype(F32), axis=0, keepdims=True)
        cg[...] = mm_t(g, wo[l]).astype(BF16)

        def pair(hp, carry):
            lo = hp * 128
            q = proj[l, :, lanes(lo, 128)]
            kk = jnp.concatenate([proj[l, :, lanes(768 + lo, 128)], kvo[l, :, lanes(lo, 128)]], 0)
            vv = jnp.concatenate(
                [proj[l, :, lanes(1536 + lo, 128)], kvo[l, :, lanes(768 + lo, 128)]], 0
            )
            kt = kk.T
            c = cg[:, lanes(lo, 128)]
            dqs = []
            dv = jnp.zeros((512, 128), F32)
            dk = jnp.zeros((512, 128), F32)
            for j in range(2):
                p = prob[l, 2 * hp + j]
                cj = c * head_mask[j]
                at = mm_t(vv, cj)
                pf = p.astype(F32)
                ds = (pf * (at - jnp.sum(at * pf, axis=0, keepdims=True))).astype(BF16)
                dv = dv + mm(p, cj)
                dk = dk + mm(ds, q * head_scaled[j])
                dqs.append(mm(kt[64 * j : 64 * (j + 1)], ds))
            pga[:, lanes(lo, 128)] = (jnp.concatenate(dqs, 0).T * 0.125).astype(BF16)
            pga[:, lanes(768 + lo, 128)] = dk[:256].astype(BF16)
            pga[:, lanes(1536 + lo, 128)] = dv[:256].astype(BF16)
            dks[:, lanes(lo, 128)] = dk[256:].astype(BF16)
            dks[:, lanes(768 + lo, 128)] = dv[256:].astype(BF16)
            return carry

        lax.fori_loop(0, 6, pair, 0)
        exchange = remote(dks, dkr.at[l], dks_sem.at[l], dkr_sem.at[l], partner)
        exchange.start()
        lt[0] = xa[l].T
        lt[1] = ctx[l].T
        exchange.wait()
        pga[:, 768:] = (pga[:, 768:].astype(F32) + dkr[l].astype(F32)).astype(BF16)
        smo[8 + 2 * l : 9 + 2 * l, :] = jnp.sum(pga[:, :768].astype(F32), axis=0, keepdims=True)
        smo[9 + 2 * l : 10 + 2 * l, :] = jnp.sum(pga[:, 1536:].astype(F32), axis=0, keepdims=True)
        dxs[...] = mm_t(pga[...], wq[l])
        hg = norm_back(s, g)

        def grads():
            for n in range(4):
                slot = n % 2
                if len(pb_copies) >= 2:
                    pb_copies[-2].wait()

                def step(i, carry):
                    if n < 3:
                        out = mm(lt[0], pga[:, lanes(768 * n + 256 * i, 256)])
                    else:
                        out = mm(lt[1], gbuf[s, :, lanes(256 * i, 256)])
                    pb[slot, :, :, lanes(256 * i, 256)] = out.astype(BF16).reshape(8, 96, 256)
                    return carry

                lax.fori_loop(0, 3, step, 0)
                copy = pltpu.make_async_copy(
                    pb.at[slot], pao.at[l, :, :, pl.ds(768 * n, 768)], pb_sem.at[slot]
                )
                copy.start()
                pb_copies.append(copy)

        return hg, grads

    hg, grads = attn_back(1)
    gbuf[1] = hg.astype(BF16)
    sent2 = push_all(gbuf.at[1], g2o, 2)
    grads()

    g = gbuf[1].astype(F32)
    g_first = (g * is_first).astype(BF16)
    g_second = (g[192:256] * is_second[192:256]).astype(BF16)
    sum_first = jnp.sum(g_first.astype(F32), axis=0, keepdims=True)
    sum_second = jnp.sum(g_second.astype(F32), axis=0, keepdims=True)
    smo[26:27, :] = jnp.where(k == 0, sum_first, 0.0)
    smo[27:28, :] = jnp.where(k == 0, sum_second, sum_first)
    loads["u3"].wait()
    loads["d3"].wait()
    dxs[...] = ffn_back(g_first, k, k, act, dg1)
    dxs[192:256, :] = dxs[192:256, :] + ffn_back(g_second, 1, 1, acts, dg1s)
    gbuf[0] = norm_back(1, gbuf[1]).astype(BF16)

    hg, grads = attn_back(0)
    hbuf[0] = hg.astype(BF16)
    fsend_a = remote(hbuf.at[4], full.at[k], fs_sem, fr_sem, partner)
    fsend_b = remote(hbuf.at[0], full.at[k], fs_sem, fr_sem, partner)

    @pl.when(k == 1)
    def _():
        fsend_a.start()
        full[1] = hbuf[0]

    @pl.when(k == 0)
    def _():
        fsend_b.start()
        full[0] = hbuf[4]

    grads()
    fsend_a.wait()

    spot = lax.broadcasted_iota(jnp.int32, (128, 128), 0)
    col = lax.broadcasted_iota(jnp.int32, (128, 128), 1)
    everything = full[...].reshape(512, 768)
    for d in range(4):
        target = (seg + d) % 4
        at = spot + 128 * target
        code = ((col == 16 + at // 32) | (col == 32 + at % 32)).astype(F32).astype(BF16)
        pick = (mm_t(code, ohv[...]) > 1.5).astype(F32).astype(BF16)
        pieces[d] = mm(pick, everything).astype(BF16)
        if d > 0:
            remote(
                pieces.at[d], comb.at[k, x], us_sem.at[d], ur_sem.at[k, x], (target, 2 * z + y)
            ).start()
        else:
            far = remote(pieces.at[0], comb.at[k, x], us_sem.at[0], ur_sem.at[k, x], partner)
            near = pltpu.make_async_copy(pieces.at[0], comb.at[k, x], us_sem.at[0])

            @pl.when(k == y)
            def _():
                near.start()

            @pl.when(k != y)
            def _():
                far.start()

    for d in range(4):
        if d > 0:
            remote(
                pieces.at[d], comb.at[k, x], us_sem.at[d], ur_sem.at[k, x], partner
            ).wait_send()
        else:
            @pl.when(k == y)
            def _():
                near.wait()

            @pl.when(k != y)
            def _():
                far.wait_send()

    for j in range(2):
        for m in range(2):
            @pl.when(jnp.logical_not((2 * k + m == seg) & (j == k)))
            def _():
                remote(
                    pieces.at[0], comb.at[j, m], us_sem.at[0], ur_sem.at[j, m], partner
                ).wait_recv()

    for local, copies in (sent1, sent3, sent2):
        local.wait()
        for copy in copies:
            copy.wait()
    for copy in pb_copies[-2:]:
        copy.wait()


def run_chain(tok, cot, oh, gb, sm, ub, wq, wo, wu, wd):
    any_ = pl.BlockSpec(memory_space=pl.ANY)
    vm = pl.BlockSpec(memory_space=pltpu.VMEM)
    dma = pltpu.SemaphoreType.DMA
    shape = jax.ShapeDtypeStruct
    return pl.pallas_call(
        chain_kernel,
        out_shape=(
            shape((4, 256, 768), BF16),
            shape((4, 256, 768), BF16),
            shape((4, 256, 768), BF16),
            shape((4, 256, 768), BF16),
            shape((2, 8, 96, 3072), BF16),
            shape((2, 2, 128, 768), BF16),
            shape((32, 768), F32),
        ),
        in_specs=[any_, any_, any_, vm, vm, vm, any_, any_, any_, any_],
        out_specs=(any_, any_, any_, any_, any_, any_, vm),
        scratch_shapes=[
            pltpu.VMEM((2, 768, 2304), BF16),
            pltpu.VMEM((2, 768, 768), BF16),
            pltpu.VMEM((2, 768, 3072), BF16),
            pltpu.VMEM((2, 3072, 768), BF16),
            pltpu.VMEM((5, 256, 768), BF16),
            pltpu.VMEM((2, 256, 768), BF16),
            pltpu.VMEM((2, 256, 2304), BF16),
            pltpu.VMEM((2, 256, 1536), BF16),
            pltpu.VMEM((2, 256, 768), BF16),
            pltpu.VMEM((2, 12, 512, 256), BF16),
            pltpu.VMEM((512, 256), F32),
            pltpu.VMEM((256, 768), BF16),
            pltpu.VMEM((256, 768), BF16),
            pltpu.VMEM((256, 3072), BF16),
            pltpu.VMEM((64, 3072), BF16),
            pltpu.VMEM((256, 3072), BF16),
            pltpu.VMEM((64, 3072), BF16),
            pltpu.VMEM((256, 3072), BF16),
            pltpu.VMEM((4, 256, 768), BF16),
            pltpu.VMEM((256, 768), BF16),
            pltpu.VMEM((256, 2304), BF16),
            pltpu.VMEM((256, 1536), BF16),
            pltpu.VMEM((2, 256, 1536), BF16),
            pltpu.VMEM((2, 768, 256), BF16),
            pltpu.VMEM((2, 8, 96, 768), BF16),
            pltpu.VMEM((256, 768), F32),
            pltpu.VMEM((2, 256, 768), BF16),
            pltpu.VMEM((4, 128, 768), BF16),
            pltpu.VMEM((4, 8, 768), F32),
            pltpu.VMEM((512, 128), BF16),
            dma((10,)), dma((2,)), dma((3,)), dma((3,)), dma((2,)), dma((2,)),
            dma((2,)), dma((2,)), dma((2,)), dma((2,)), dma((2,)),
            dma((2,)), dma((2,)), dma((3, 3)), dma((3, 3)), dma((3,)), dma((2,)),
            dma(()), dma(()), dma((4,)), dma((2, 2)), dma(()),
        ],
        compiler_params=pltpu.CompilerParams(
            collective_id=0, has_side_effects=True, vmem_limit_bytes=62 * MIB
        ),
    )(tok, cot, oh, gb, sm, ub, wq, wo, wu, wd)


def rolled_inputs(tokens, group_ids, type_ids, out_cotangent):
    rows = tokens.shape[1]
    spots = jnp.arange(rows, dtype=jnp.int32)
    starts = jnp.min(jnp.where(type_ids == 0, spots[None, :], rows), axis=1)
    tok, cot, oh = [], [], []
    lanes_at = jnp.arange(128, dtype=jnp.int32)[None, :]
    for m in range(tokens.shape[0]):
        s = starts[m]
        turn = lambda v: lax.dynamic_slice_in_dim(jnp.concatenate([v, v], 0), s, rows, 0)
        tok.append(turn(tokens[m]))
        cot.append(turn(out_cotangent[m]))
        gid = turn(group_ids[m])[:, None]
        spot = ((spots + s) % rows)[:, None]
        oh.append(
            (lanes_at == gid) | (lanes_at == 16 + spot // 32) | (lanes_at == 32 + spot % 32)
        )
    return jnp.stack(tok), jnp.stack(cot), jnp.stack(oh).astype(BF16)


def fast_device(
    tokens, group_ids, type_ids, norm_gain, norm_bias, qkv_weight, qv_bias, out_weight,
    out_bias, up_weight, up_bias, down_weight, down_bias, out_cotangent,
):
    seg = lax.axis_index("segment")
    dp = lax.axis_index("dp")
    tok, cot, oh = rolled_inputs(tokens, group_ids, type_ids, out_cotangent)
    gb = jnp.concatenate([norm_gain, norm_bias, jnp.zeros((6, D), BF16)], 0).astype(F32)
    sm = jnp.concatenate(
        [qv_bias.reshape(4, D), out_bias, jnp.zeros((2, D), BF16), down_bias,
         jnp.zeros((5, D), BF16)], 0
    ).astype(F32)
    ub = up_bias.astype(F32).reshape(36, 1, 256)
    x1, x3, g2, c4, pa, comb, smo = run_chain(
        tok, cot, oh, gb, sm, ub, qkv_weight, out_weight, up_weight, down_weight
    )
    k = dp % 2
    us = lax.dynamic_slice_in_dim(up_weight, seg * 768, 768, 2)
    ds = lax.dynamic_slice_in_dim(down_weight, seg * 768, 768, 1)
    bs = lax.dynamic_slice_in_dim(up_bias, seg * 768, 768, 1).astype(F32)
    img = (jnp.arange(256)[None, :] < PATCHES) & (k == 0)
    img = jnp.broadcast_to(img, (4, 256)).reshape(1024)
    ups, downs = [], []
    for e in range(3):
        xs = (x3 if e == 2 else x1).reshape(1024, 768)
        gs = (c4 if e == 2 else g2).reshape(1024, 768)
        if e < 2:
            gs = jnp.where((img == (e == 0))[:, None], gs, 0)
        a, slope = gelu_both(mm(xs, us[e]) + bs[e])
        pg = (mm_t(gs, ds[e]) * slope).astype(BF16)
        ups.append(mm(xs.T, pg))
        downs.append(mm(a.astype(BF16).T, gs))
    up = lax.all_gather(lax.psum(jnp.stack(ups), "dp").astype(BF16), "segment", axis=2, tiled=True)
    down = lax.all_gather(lax.psum(jnp.stack(downs), "dp").astype(BF16), "segment", axis=1, tiled=True)
    cut = lambda v, n, ax: lax.dynamic_slice_in_dim(v, dp * n, n, ax).astype(F32)
    att = lax.psum(pa.astype(F32), ("segment", "dp"))
    att = lax.dynamic_index_in_dim(att, dp, 1, keepdims=False)
    sm_all = lax.psum(smo, ("segment", "dp"))
    mine = cut(sm_all, 96, 1)
    upb = cut(sm_all[14:26].reshape(3, 3072), 384, 1)
    return (
        comb[0],
        comb[1].astype(F32),
        lax.dynamic_slice_in_dim(mine, seg, 1, 0),
        lax.dynamic_slice_in_dim(mine, 4 + seg, 1, 0),
        att[:, :, :2304],
        mine[8:12].reshape(2, 2, 96),
        att[:, :, 2304:],
        mine[12:14],
        cut(up, 96, 1),
        upb,
        cut(down, 384, 1),
        mine[26:29],
    )


def solution(mesh):
    known = mesh.shape["segment"] == 4 and mesh.shape["dp"] == 8
    return jax.shard_map(
        fast_device if known else per_device,
        mesh=mesh,
        in_specs=(
            P("dp", None, None),
            P("dp", None),
            P("dp", None),
            P("segment", None),
            P("segment", None),
            P(),
            P(),
            P(),
            P(),
            P(),
            P(),
            P(),
            P(),
            P("dp", None, None),
        ),
        out_specs=(
            P("dp", "segment", None),
            P("dp", "segment", None),
            P("segment", "dp"),
            P("segment", "dp"),
            P(None, "dp", None),
            P(None, None, "dp"),
            P(None, "dp", None),
            P(None, "dp"),
            P(None, "dp", None),
            P(None, "dp"),
            P(None, "dp", None),
            P(None, "dp"),
        ),
        check_vma=False,
    )
```

```python
from functools import partial
import math

import jax
import jax.numpy as jnp
from jax import lax
from jax.experimental import pallas as pl
from jax.experimental.pallas import tpu as pltpu
from jax.sharding import PartitionSpec as P

D = 768
H = 12
HD = 64
FF = 3072
PATCHES = 197


def shortened(value):

    def short(part):
        return part.astype(jnp.bfloat16) if part.dtype == jnp.float32 else part

    return jax.tree.map(short, value)


def shifted_2(value, axis, steps):
    count = lax.axis_size(axis)
    leading, last = (max(0, -steps), min(count, count - steps))
    return lax.ppermute(value, axis, [(source, source + steps) for source in range(leading, last)])


def spread_2(value, axis, root):
    mine = lax.axis_index(axis) == root
    return lax.psum(jnp.where(mine, value, jnp.zeros_like(value)), axis)


def normalize(values, scale_row, shift_row):
    center = values - jnp.mean(values, axis=-1, keepdims=True)
    spread = jnp.mean(center * center, axis=-1, keepdims=True)
    return center * lax.rsqrt(spread + 1e-05) * scale_row + shift_row


def smooth_gelu(values):
    return (
        0.5
        * values
        * (1.0 + jnp.tanh(0.7978845608028654 * (values + 0.044715 * values * values * values)))
    )


def text_rows(image_start, row_count):
    text_spots = jnp.arange(row_count - PATCHES, dtype=jnp.int32)
    return text_spots + jnp.where(text_spots >= image_start, PATCHES, 0).astype(jnp.int32)


def split_routes(values, image_start, text_index):
    return (
        lax.dynamic_slice_in_dim(values, image_start, PATCHES, 0),
        jnp.take(values, text_index, axis=0),
    )


def place_rows(image_part, text_part, image_start, text_index):
    merged = jnp.zeros(
        (image_part.shape[0] + text_part.shape[0], image_part.shape[1]), image_part.dtype
    )
    merged = merged.at[text_index].set(text_part)
    return lax.dynamic_update_slice_in_dim(merged, image_part, image_start, 0)


def attention_forward(hidden, same_group, scale_row, shift_row, weight_set):
    qkv_proj, qv_shift, out_proj, out_shift = weight_set
    row_count = hidden.shape[0]
    attn_in = normalize(hidden, scale_row, shift_row).astype(jnp.bfloat16)
    zero_bias = jnp.zeros((D,), jnp.float32)
    bias_row = jnp.concatenate(
        [qv_shift[0].astype(jnp.float32), zero_bias, qv_shift[1].astype(jnp.float32)]
    )
    projected = (jnp.dot(attn_in, qkv_proj, preferred_element_type=jnp.float32) + bias_row).astype(
        jnp.bfloat16
    )
    queries = projected[:, :D].reshape(row_count, H, HD)
    keys_part = projected[:, D : 2 * D].reshape(row_count, H, HD)
    values_part = projected[:, 2 * D :].reshape(row_count, H, HD)
    scores = jnp.einsum(
        "qhd,khd->hqk", queries, keys_part, preferred_element_type=jnp.float32
    ) * HD ** (-0.5)
    scores = jnp.where(same_group[None], scores, -1e30)
    shifted = scores - jnp.max(scores, axis=-1, keepdims=True)
    exponent = jnp.exp(shifted)
    attention = exponent / jnp.sum(exponent, axis=-1, keepdims=True)
    attention_low = attention.astype(jnp.bfloat16)
    context = jnp.einsum(
        "hqk,khd->qhd", attention_low, values_part, preferred_element_type=jnp.float32
    )
    context = context.reshape(row_count, D).astype(jnp.bfloat16)
    result_block = hidden + (
        jnp.dot(context, out_proj, preferred_element_type=jnp.float32)
        + out_shift.astype(jnp.float32)
    )
    return (
        result_block,
        (attn_in, queries, keys_part, values_part, attention, attention_low, context),
    )


def attention_backward(grad_low, hidden, same_group, scale_row, shift_row, weight_set):
    qkv_proj, qv_shift, out_proj, out_shift = weight_set
    _, kept_values = attention_forward(hidden, same_group, scale_row, shift_row, weight_set)
    attn_in, queries, keys_part, values_part, attention, attention_low, context = kept_values
    row_count = hidden.shape[0]
    grad_out = grad_low.astype(jnp.float32)
    out_proj_grad = jnp.einsum("rd,re->de", context, grad_low, preferred_element_type=jnp.float32)
    out_shift_grad = jnp.sum(grad_out, axis=0)
    context_grad = jnp.einsum("re,de->rd", grad_low, out_proj, preferred_element_type=jnp.float32)
    context_grad = context_grad.astype(jnp.bfloat16).reshape(row_count, H, HD)
    values_grad = jnp.einsum(
        "hqk,qhd->khd", attention_low, context_grad, preferred_element_type=jnp.float32
    )
    attention_grad = jnp.einsum(
        "qhd,khd->hqk", context_grad, values_part, preferred_element_type=jnp.float32
    )
    scores_grad = attention * (
        attention_grad - jnp.sum(attention_grad * attention, axis=-1, keepdims=True)
    )
    scores_grad = scores_grad.astype(jnp.bfloat16)
    queries_grad = jnp.einsum(
        "hqk,khd->qhd", scores_grad, keys_part, preferred_element_type=jnp.float32
    ) * HD ** (-0.5)
    keys_grad = jnp.einsum(
        "hqk,qhd->khd", scores_grad, queries, preferred_element_type=jnp.float32
    ) * HD ** (-0.5)
    projected_grad = jnp.concatenate(
        [
            queries_grad.reshape(row_count, D),
            keys_grad.reshape(row_count, D),
            values_grad.reshape(row_count, D),
        ],
        axis=1,
    ).astype(jnp.bfloat16)
    qv_shift_grad = jnp.stack(
        [
            jnp.sum(projected_grad[:, :D].astype(jnp.float32), axis=0),
            jnp.sum(projected_grad[:, 2 * D :].astype(jnp.float32), axis=0),
        ]
    )
    qkv_proj_grad = jnp.einsum(
        "rd,re->de", attn_in, projected_grad, preferred_element_type=jnp.float32
    )
    attn_in_grad = jnp.einsum(
        "re,de->rd", projected_grad, qkv_proj, preferred_element_type=jnp.float32
    )
    hidden_part, scale_grad, shift_grad = jax.vjp(normalize, hidden, scale_row, shift_row)[1](
        attn_in_grad
    )
    return (
        grad_out + hidden_part,
        [scale_grad, shift_grad, qkv_proj_grad, qv_shift_grad, out_proj_grad, out_shift_grad],
    )


def expert_inputs(ffn_in, image_start, routed):
    row_count = ffn_in.shape[0]
    text_index = text_rows(image_start, row_count)
    if not routed:
        return ((ffn_in,), text_index)
    return (split_routes(ffn_in, image_start, text_index), text_index)


def expert_forward(hidden, image_start, scale_row, shift_row, weight_set):
    up_proj, up_shift, down_proj, down_shift, routed = weight_set
    ffn_in = normalize(hidden, scale_row, shift_row).astype(jnp.bfloat16)
    inputs, text_index = expert_inputs(ffn_in, image_start, routed)
    pre_acts = tuple(
        (
            jnp.dot(inputs[expert], up_proj[expert], preferred_element_type=jnp.float32)
            + up_shift[expert].astype(jnp.float32)
            for expert in range(len(inputs))
        )
    )
    activated = tuple((smooth_gelu(pre_act).astype(jnp.bfloat16) for pre_act in pre_acts))
    expert_outs = tuple(
        (
            jnp.dot(activated[expert], down_proj[expert], preferred_element_type=jnp.float32)
            + down_shift[expert].astype(jnp.float32)
            for expert in range(len(inputs))
        )
    )
    if not routed:
        joined = expert_outs[0]
    else:
        joined = place_rows(expert_outs[0], expert_outs[1], image_start, text_index)
    return (hidden + joined, (inputs, pre_acts, activated, text_index))


def expert_backward(grad_low, hidden, image_start, scale_row, shift_row, weight_set):
    up_proj, up_shift, down_proj, down_shift, routed = weight_set
    _, kept_values = expert_forward(hidden, image_start, scale_row, shift_row, weight_set)
    inputs, pre_acts, activated, text_index = kept_values
    grad_out = grad_low.astype(jnp.float32)
    if not routed:
        grad_parts = (grad_low,)
    else:
        grad_parts = split_routes(grad_low, image_start, text_index)
    up_grads, up_shift_grads, down_grads, down_shift_grads, input_grads = ([], [], [], [], [])
    for expert in range(len(inputs)):
        expert_grad = grad_parts[expert]
        down_grads.append(
            jnp.einsum(
                "rf,rd->fd", activated[expert], expert_grad, preferred_element_type=jnp.float32
            )
        )
        down_shift_grads.append(jnp.sum(expert_grad.astype(jnp.float32), axis=0))
        act_grad = jnp.einsum(
            "rd,fd->rf", expert_grad, down_proj[expert], preferred_element_type=jnp.float32
        )
        pre_grad = jax.vjp(smooth_gelu, pre_acts[expert])[1](act_grad)[0].astype(jnp.bfloat16)
        up_grads.append(
            jnp.einsum("rd,rf->df", inputs[expert], pre_grad, preferred_element_type=jnp.float32)
        )
        up_shift_grads.append(jnp.sum(pre_grad.astype(jnp.float32), axis=0))
        input_grads.append(
            jnp.einsum("rf,df->rd", pre_grad, up_proj[expert], preferred_element_type=jnp.float32)
        )
    if not routed:
        ffn_in_grad = input_grads[0]
    else:
        ffn_in_grad = place_rows(input_grads[0], input_grads[1], image_start, text_index)
    hidden_part, scale_grad, shift_grad = jax.vjp(normalize, hidden, scale_row, shift_row)[1](
        ffn_in_grad
    )
    return (
        grad_out + hidden_part,
        [
            scale_grad,
            shift_grad,
            jnp.stack(up_grads),
            jnp.stack(up_shift_grads),
            jnp.stack(down_grads),
            jnp.stack(down_shift_grads),
        ],
    )


def attention_layout():
    return [((D,), 0), ((D,), 0), ((D, 3 * D), 0), ((2, D), 1), ((D, D), 0), ((D,), 0)]


def expert_layout(experts_here):
    return [
        ((D,), 0),
        ((D,), 0),
        ((experts_here, D, FF), 1),
        ((experts_here, FF), 1),
        ((experts_here, FF, D), 1),
        ((experts_here, D), 1),
    ]


def section_layouts():
    return [attention_layout(), expert_layout(2), attention_layout(), expert_layout(1)]


def layout_entries(layout):
    return sum((math.prod(full_shape) for full_shape, split_dim in layout))


def padded_width(entries):
    return -(-entries // 128) * 128


def split_rows(grad_term, split_dim, group_count):
    full_shape = grad_term.shape
    pieces_all = grad_term.reshape(
        full_shape[:split_dim]
        + (group_count, full_shape[split_dim] // group_count)
        + full_shape[split_dim + 1 :]
    )
    return jnp.moveaxis(pieces_all, split_dim, 0).reshape(group_count, -1)


def fit_width(flat_terms, width):
    return jnp.pad(flat_terms, ((0, 0), (0, width - flat_terms.shape[1])))


def pack_terms(grad_terms, layout, group_count, pack_width):
    flat_terms = jnp.concatenate(
        [
            split_rows(grad_term, split_dim, group_count)
            for grad_term, (full_shape, split_dim) in zip(grad_terms, layout)
        ],
        axis=1,
    )
    return fit_width(flat_terms, pack_width)


def unpack_row(flat_row, layout, group_count):
    results = []
    offset = 0
    for full_shape, split_dim in layout:
        shard_shape = (
            full_shape[:split_dim]
            + (full_shape[split_dim] // group_count,)
            + full_shape[split_dim + 1 :]
        )
        entries = math.prod(shard_shape)
        results.append(flat_row[offset : offset + entries].reshape(shard_shape))
        offset = offset + entries
    return results


def per_device(
    tokens,
    group_ids,
    type_ids,
    norm_gain,
    norm_bias,
    qkv_weight,
    qv_bias,
    out_weight,
    out_bias,
    up_weight,
    up_bias,
    down_weight,
    down_bias,
    out_cotangent,
):
    segment_count = lax.axis_size("segment")
    segment_place = lax.axis_index("segment")
    group_count = lax.axis_size("dp")
    micro_count = tokens.shape[0]
    row_count = tokens.shape[1]
    tick_count = micro_count + segment_count - 1
    scale_row = norm_gain[0].astype(jnp.float32)
    shift_row = norm_bias[0].astype(jnp.float32)
    layouts = section_layouts()
    pack_width = padded_width(max((layout_entries(layout) for layout in layouts)) // group_count)
    same_all = group_ids[:, :, None] == group_ids[:, None, :]
    row_spots = jnp.arange(row_count, dtype=jnp.int32)[None, :]
    image_starts = jnp.min(jnp.where(type_ids == 0, row_spots, row_count), axis=1)
    attention_sets = tuple(
        (
            (
                qkv_weight[layer_index],
                qv_bias[layer_index],
                out_weight[layer_index],
                out_bias[layer_index],
            )
            for layer_index in range(2)
        )
    )
    expert_sets = (
        (up_weight[0:2], up_bias[0:2], down_weight[0:2], down_bias[0:2], True),
        (up_weight[2:3], up_bias[2:3], down_weight[2:3], down_bias[2:3], False),
    )

    def forward_branch(section, block_in, position):
        if section % 2 == 0:
            result_block = attention_forward(
                block_in, same_all[position], scale_row, shift_row, attention_sets[section // 2]
            )[0]
        else:
            result_block = expert_forward(
                block_in, image_starts[position], scale_row, shift_row, expert_sets[section // 2]
            )[0]
        return result_block.astype(jnp.bfloat16)

    def forward_tick(tick_index, loop_state):
        incoming, kept_inputs, finals = loop_state
        micro_index = tick_index - segment_place
        active = (micro_index >= 0) & (micro_index < micro_count)
        position = jnp.clip(micro_index, 0, micro_count - 1)
        given_block = jnp.where(segment_place == 0, tokens[position], incoming)

        def forward_compute(block_in):
            return lax.switch(
                segment_place,
                [partial(forward_branch, section) for section in range(segment_count)],
                block_in.astype(jnp.float32),
                position,
            )

        def forward_resting(block_in):
            return jnp.zeros_like(block_in)

        result_block = lax.cond(active, forward_compute, forward_resting, given_block)
        kept_inputs = kept_inputs.at[position].set(
            jnp.where(active, given_block, kept_inputs[position])
        )
        finals = finals.at[position].set(jnp.where(active, result_block, finals[position]))
        incoming = jax.tree.map(
            lambda part, own: part.astype(own.dtype),
            shifted_2(shortened(result_block), "segment", 1),
            result_block,
        )
        return (incoming, kept_inputs, finals)

    zero_block = jnp.zeros(tokens.shape[1:], jnp.bfloat16)
    stash_zero = jnp.zeros(tokens.shape, jnp.bfloat16)
    _, kept_inputs, finals = lax.fori_loop(
        0, tick_count, forward_tick, (zero_block, stash_zero, stash_zero)
    )

    def backward_branch(section, grad_low, position):
        hidden = kept_inputs[position].astype(jnp.float32)
        if section % 2 == 0:
            hidden_grad, grad_terms = attention_backward(
                grad_low,
                hidden,
                same_all[position],
                scale_row,
                shift_row,
                attention_sets[section // 2],
            )
        else:
            hidden_grad, grad_terms = expert_backward(
                grad_low,
                hidden,
                image_starts[position],
                scale_row,
                shift_row,
                expert_sets[section // 2],
            )
        return (hidden_grad, pack_terms(grad_terms, layouts[section], group_count, pack_width))

    def backward_tick(tick_index, loop_state):
        incoming, input_grads, totals = loop_state
        micro_index = tick_index - (segment_count - 1 - segment_place)
        active = (micro_index >= 0) & (micro_index < micro_count)
        position = jnp.clip(micro_index, 0, micro_count - 1)
        given_block = jnp.where(
            segment_place == segment_count - 1, out_cotangent[position], incoming
        )

        def backward_compute(block_in):
            return lax.switch(
                segment_place,
                [partial(backward_branch, section) for section in range(segment_count)],
                block_in,
                position,
            )

        def backward_resting(block_in):
            return (
                jnp.zeros(block_in.shape, jnp.float32),
                jnp.zeros((group_count, pack_width), jnp.float32),
            )

        hidden_grad, flat_terms = lax.cond(active, backward_compute, backward_resting, given_block)
        input_grads = input_grads.at[position].set(
            jnp.where(active, hidden_grad, input_grads[position])
        )
        totals = totals + flat_terms
        incoming = shifted_2(hidden_grad.astype(jnp.bfloat16), "segment", -1)
        return (incoming, input_grads, totals)

    grads_zero = jnp.zeros(tokens.shape, jnp.float32)
    totals_start = jnp.zeros((group_count, pack_width), jnp.float32)
    _, input_grads, totals = lax.fori_loop(
        0, tick_count, backward_tick, (zero_block, grads_zero, totals_start)
    )
    width_d = D // group_count
    shares = lax.psum_scatter(totals, "dp", scatter_dimension=0, tiled=True)
    gathered = lax.all_gather(shares.astype(jnp.bfloat16), "segment", axis=0, tiled=True).astype(
        shares.dtype
    )
    norm_gain_grad = shares[0, :width_d].reshape(1, width_d)
    norm_bias_grad = shares[0, width_d : 2 * width_d].reshape(1, width_d)
    first_attention = unpack_row(gathered[0], layouts[0], group_count)
    both_experts = unpack_row(gathered[1], layouts[1], group_count)
    second_attention = unpack_row(gathered[2], layouts[2], group_count)
    uniting_expert = unpack_row(gathered[3], layouts[3], group_count)
    qkv_weight_grad = jnp.stack([first_attention[2], second_attention[2]])
    qv_bias_grad = jnp.stack([first_attention[3], second_attention[3]])
    out_weight_grad = jnp.stack([first_attention[4], second_attention[4]])
    out_bias_grad = jnp.stack([first_attention[5], second_attention[5]])
    up_weight_grad = jnp.concatenate([both_experts[2], uniting_expert[2]], axis=0)
    up_bias_grad = jnp.concatenate([both_experts[3], uniting_expert[3]], axis=0)
    down_weight_grad = jnp.concatenate([both_experts[4], uniting_expert[4]], axis=0)
    down_bias_grad = jnp.concatenate([both_experts[5], uniting_expert[5]], axis=0)
    own_rows = row_count // segment_count
    final_all = spread_2(finals, "segment", segment_count - 1)
    input_all = spread_2(input_grads.astype(jnp.bfloat16), "segment", 0).astype(input_grads.dtype)
    layer_output = lax.dynamic_slice_in_dim(final_all, segment_place * own_rows, own_rows, 1)
    input_grad = lax.dynamic_slice_in_dim(input_all, segment_place * own_rows, own_rows, 1)
    return (
        layer_output,
        input_grad,
        norm_gain_grad,
        norm_bias_grad,
        qkv_weight_grad,
        qv_bias_grad,
        out_weight_grad,
        out_bias_grad,
        up_weight_grad,
        up_bias_grad,
        down_weight_grad,
        down_bias_grad,
    )


F32 = jnp.float32
BF16 = jnp.bfloat16
MESH = pl.DeviceIdType.MESH
MIB = 2**20


def mm(a, b):
    return lax.dot_general(a, b, (((1,), (0,)), ((), ())), preferred_element_type=F32)


def mm_t(a, b):
    return lax.dot_general(a, b, (((1,), (1,)), ((), ())), preferred_element_type=F32)


def ln_parts(h):
    center = h - jnp.mean(h, axis=-1, keepdims=True)
    r = lax.rsqrt(jnp.mean(center * center, axis=-1, keepdims=True) + 1e-05)
    return center * r, r


def gelu_both(x):
    x2 = x * x
    t = jnp.tanh(0.7978845608028654 * (x + 0.044715 * x2 * x))
    half = 0.5 * (1.0 + t)
    slope = half + (0.5 * x) * (1.0 - t * t) * (
        0.7978845608028654 + (3.0 * 0.044715 * 0.7978845608028654) * x2
    )
    return x * half, slope


def places():
    seg = lax.axis_index("segment")
    dp = lax.axis_index("dp")
    return seg, dp, dp // 2, dp % 2, seg // 2, seg % 2


def chain_kernel(
    tok, cot, oh, gb, sm, ub, wq_h, wo_h, wu_h, wd_h,
    x1o, x3o, g2o, c4o, pao, comb, smo,
    wq, wo, wu, wd, hbuf, xa, proj, kvo, ctx, prob, bias, xf1, xf3, act, acts, dg1, dg1s, dg3,
    gbuf, cg, pga, dks, dkr, lt, pb, dxs, full, pieces, gball, ohv,
    w_sem, in_sem, gs_sem, gr_sem, ts_sem, tr_sem, c_sem, cs_sem, cr_sem, kvs_sem, kvr_sem,
    dks_sem, dkr_sem, as_sem, ar_sem, al_sem, pb_sem, fs_sem, fr_sem, us_sem, ur_sem, g4_sem,
):
    seg, dp, z, k, y, x = places()
    other = 1 - k
    partner = (seg, 2 * z + other)

    def peer(d):
        return ((seg + d) % 4, dp)

    def back(d):
        return (seg + 4 - d) % 4

    loads = {}

    def load(name, src, dst, sem):
        copy = pltpu.make_async_copy(src, dst, sem)
        copy.start()
        loads[name] = copy

    load("q0", wq_h.at[0], wq.at[0], w_sem.at[0])
    load("o0", wo_h.at[0], wo.at[0], w_sem.at[1])

    barrier = pltpu.get_barrier_semaphore()
    for d in range(4):
        for c in range(2):
            if d == 0 and c == 1:
                continue
            where = partner if d == 0 else ((seg + d) % 4, 2 * z + c)
            pl.semaphore_signal(barrier, inc=1, device_id=where, device_id_type=MESH)
    pl.semaphore_wait(barrier, 7)

    def remote(src, dst, ssem, rsem, where):
        return pltpu.make_async_remote_copy(
            src_ref=src, dst_ref=dst, send_sem=ssem, recv_sem=rsem,
            device_id=where, device_id_type=MESH,
        )

    own_tok = pl.ds(pl.multiple_of(256 * k, 256), 256)
    far_tok = pl.ds(pl.multiple_of(256 * other, 256), 256)
    tok_here = pltpu.make_async_copy(tok.at[x, own_tok], hbuf.at[0], in_sem.at[0])
    oh_here = pltpu.make_async_copy(oh.at[x], ohv, in_sem.at[1])
    tok_far = remote(tok.at[x, far_tok], hbuf.at[0], ts_sem.at[0], tr_sem.at[0], partner)
    oh_far = remote(oh.at[x], ohv, ts_sem.at[1], tr_sem.at[1], partner)

    @pl.when(k == y)
    def _():
        tok_here.start()
        oh_here.start()
        tok_far.start()
        oh_far.start()

    gains = [
        remote(gb, gball.at[seg], gs_sem.at[d - 1], gr_sem.at[d - 1], peer(d)) for d in (1, 2, 3)
    ]
    for copy in gains:
        copy.start()
    load("u0", wu_h.at[0], wu.at[0], w_sem.at[2])
    load("u1", wu_h.at[1], wu.at[1], w_sem.at[3])
    load("d0", wd_h.at[0], wd.at[0], w_sem.at[4])
    load("d1", wd_h.at[1], wd.at[1], w_sem.at[5])
    cots = []
    for m in range(2):
        here = pltpu.make_async_copy(cot.at[m, own_tok], c4o.at[2 * k + m], c_sem.at[m])
        there = remote(
            cot.at[m, far_tok], c4o.at[2 * k + m], cs_sem.at[m], cr_sem.at[m], partner
        )
        here.start()
        there.start()
        cots.append((here, there))
    load("q1", wq_h.at[1], wq.at[1], w_sem.at[6])
    load("o1", wo_h.at[1], wo.at[1], w_sem.at[7])

    gball[seg] = gb[...]
    smo[...] = jnp.zeros_like(smo)
    for copy in gains:
        copy.wait()

    @pl.when(k == y)
    def _():
        tok_here.wait()
        oh_here.wait()
        tok_far.wait_send()
        oh_far.wait_send()

    @pl.when(k != y)
    def _():
        tok_far.wait_recv()
        oh_far.wait_recv()

    group_lane = (lax.broadcasted_iota(jnp.int32, (256, 128), 1) < 3).astype(F32).astype(BF16)
    mine = ohv[own_tok, :] * group_lane
    theirs = ohv[far_tok, :]
    same = mm_t(jnp.concatenate([ohv[own_tok, :], theirs], axis=0), mine)
    bias[...] = jnp.where(same > 0.5, 0.0, -1e30)

    lane = lax.broadcasted_iota(jnp.int32, (1, 128), 1)
    head_mask = [(lane < 64).astype(F32).astype(BF16), (lane >= 64).astype(F32).astype(BF16)]
    head_scaled = [part * 0.125 for part in head_mask]

    def gain_of(s):
        return gball[s, 0:1, :], gball[s, 1:2, :]

    def normed(s):
        n, _ = ln_parts(hbuf[s].astype(F32))
        gain, shift = gain_of(s)
        return (n * gain + shift).astype(BF16)

    def lanes(start, width):
        return pl.ds(pl.multiple_of(start, 128), width)

    def attn_fwd(l):
        s = 2 * l
        xin = normed(s)
        xa[l] = xin
        loads[f"q{l}"].wait()
        kv = remote(
            proj.at[l, :, pl.ds(768, 1536)], kvo.at[l], kvs_sem.at[l], kvr_sem.at[l], partner
        )
        for n in (1, 2, 0):
            part = mm(xin, wq[l, :, 768 * n : 768 * (n + 1)])
            if n != 1:
                row = 2 * l + (n == 2)
                part = part + sm[row : row + 1, :]
            proj[l, :, 768 * n : 768 * (n + 1)] = part.astype(BF16)
            if n == 2:
                kv.start()
        kv.wait()

        def pair(hp, carry):
            lo = hp * 128
            q = proj[l, :, lanes(lo, 128)]
            kk = jnp.concatenate([proj[l, :, lanes(768 + lo, 128)], kvo[l, :, lanes(lo, 128)]], 0)
            vv = jnp.concatenate(
                [proj[l, :, lanes(1536 + lo, 128)], kvo[l, :, lanes(768 + lo, 128)]], 0
            )
            vt = vv.T
            outs = []
            for j in range(2):
                st = mm_t(kk, q * head_scaled[j]) + bias[...]
                e = jnp.exp(st - jnp.max(st, axis=0, keepdims=True))
                p = (e * (1.0 / jnp.sum(e, axis=0, keepdims=True))).astype(BF16)
                prob[l, 2 * hp + j] = p
                outs.append(mm(vt[64 * j : 64 * (j + 1)], p))
            ctx[l, :, lanes(lo, 128)] = jnp.concatenate(outs, 0).T.astype(BF16)
            return carry

        lax.fori_loop(0, 6, pair, 0)
        loads[f"o{l}"].wait()
        out = mm(ctx[l], wo[l]) + sm[4 + l : 5 + l, :]
        hbuf[s + 1] = (hbuf[s].astype(F32) + out).astype(BF16)

    def ffn_up(rows_in, slot, e, act_ref, dg_ref):
        def step(n, carry):
            at = lanes(256 * n, 256)
            pre = mm(rows_in, wu[slot, :, at]) + ub[12 * e + n]
            a, slope = gelu_both(pre)
            act_ref[:, at] = a.astype(BF16)
            dg_ref[:, at] = slope.astype(BF16)
            return carry

        lax.fori_loop(0, 12, step, 0)

    def ffn_down(act_ref, slot, e):
        return mm(act_ref[...], wd[slot]) + sm[pl.ds(8 + e, 1), :]

    row = lax.broadcasted_iota(jnp.int32, (256, 1), 0)
    is_first = ((row < PATCHES) | (k == 1)).astype(F32)
    is_second = ((row >= PATCHES) & (k == 0)).astype(F32)

    def push_all(src, dst, slot):
        local = pltpu.make_async_copy(src, dst.at[seg], al_sem.at[slot])
        local.start()
        copies = [
            remote(src, dst.at[seg], as_sem.at[slot, d - 1], ar_sem.at[slot, d - 1], peer(d))
            for d in (1, 2, 3)
        ]
        for copy in copies:
            copy.start()
        return local, copies

    attn_fwd(0)

    xf1[...] = normed(1)
    sent1 = push_all(xf1, x1o, 0)
    loads["u0"].wait()
    loads["u1"].wait()
    ffn_up(xf1[...], k, k, act, dg1)
    ffn_up(xf1[192:256, :], 1, 1, acts, dg1s)
    loads["d0"].wait()
    loads["d1"].wait()
    dxs[...] = ffn_down(act, k, k)
    second = ffn_down(acts, 1, 1)
    m2 = is_second[192:256]
    dxs[192:256, :] = jnp.where(m2 > 0.5, second, dxs[192:256, :])
    hbuf[2] = (hbuf[1].astype(F32) + dxs[...]).astype(BF16)
    load("u2", wu_h.at[2], wu.at[0], w_sem.at[8])
    load("d2", wd_h.at[2], wd.at[0], w_sem.at[9])

    attn_fwd(1)

    xf3[...] = normed(3)
    sent3 = push_all(xf3, x3o, 1)
    loads["u2"].wait()
    ffn_up(xf3[...], 0, 2, act, dg3)
    loads["d2"].wait()
    for m in range(2):
        cots[m][0].wait()
        cots[m][1].wait()
    g4 = pltpu.make_async_copy(c4o.at[seg], gbuf.at[3], g4_sem)
    g4.start()
    h4 = (hbuf[3].astype(F32) + ffn_down(act, 0, 2)).astype(BF16)
    hbuf[4] = h4
    g4.wait()

    def ffn_back(g, slot, e, act_ref, dg_ref):
        def step(n, carry):
            at = lanes(256 * n, 256)
            ag = mm_t(g, wd[slot, pl.ds(pl.multiple_of(256 * n, 256), 256), :])
            pg = (ag * dg_ref[:, at].astype(F32)).astype(BF16)
            act_ref[:, at] = pg
            spot = (pl.ds(14 + 4 * e + n // 3, 1), lanes(256 * (n % 3), 256))
            smo[spot] = smo[spot] + jnp.sum(pg.astype(F32), axis=0, keepdims=True)
            return carry

        lax.fori_loop(0, 12, step, 0)
        return mm_t(act_ref[...], wu[slot])

    def norm_back(s, g):
        n, r = ln_parts(hbuf[s].astype(F32))
        gain, _ = gain_of(s)
        dx = dxs[...]
        smo[s : s + 1, :] = jnp.sum(dx * n, axis=0, keepdims=True)
        smo[4 + s : 5 + s, :] = jnp.sum(dx, axis=0, keepdims=True)
        c = dx * gain
        return g.astype(F32) + r * (
            c - jnp.mean(c, axis=-1, keepdims=True) - n * jnp.mean(c * n, axis=-1, keepdims=True)
        )

    g = gbuf[3]
    smo[28:29, :] = jnp.sum(g.astype(F32), axis=0, keepdims=True)
    dxs[...] = ffn_back(g, 0, 2, act, dg3)
    load("u3", wu_h.at[0], wu.at[0], w_sem.at[2])
    load("d3", wd_h.at[0], wd.at[0], w_sem.at[4])
    gbuf[2] = norm_back(3, g).astype(BF16)

    pb_copies = []

    def attn_back(l):
        s = 2 * l
        g = gbuf[s]
        smo[12 + l : 13 + l, :] = jnp.sum(g.astype(F32), axis=0, keepdims=True)
        cg[...] = mm_t(g, wo[l]).astype(BF16)

        def pair(hp, carry):
            lo = hp * 128
            q = proj[l, :, lanes(lo, 128)]
            kk = jnp.concatenate([proj[l, :, lanes(768 + lo, 128)], kvo[l, :, lanes(lo, 128)]], 0)
            vv = jnp.concatenate(
                [proj[l, :, lanes(1536 + lo, 128)], kvo[l, :, lanes(768 + lo, 128)]], 0
            )
            kt = kk.T
            c = cg[:, lanes(lo, 128)]
            dqs = []
            dv = jnp.zeros((512, 128), F32)
            dk = jnp.zeros((512, 128), F32)
            for j in range(2):
                p = prob[l, 2 * hp + j]
                cj = c * head_mask[j]
                at = mm_t(vv, cj)
                pf = p.astype(F32)
                ds = (pf * (at - jnp.sum(at * pf, axis=0, keepdims=True))).astype(BF16)
                dv = dv + mm(p, cj)
                dk = dk + mm(ds, q * head_scaled[j])
                dqs.append(mm(kt[64 * j : 64 * (j + 1)], ds))
            pga[:, lanes(lo, 128)] = (jnp.concatenate(dqs, 0).T * 0.125).astype(BF16)
            pga[:, lanes(768 + lo, 128)] = dk[:256].astype(BF16)
            pga[:, lanes(1536 + lo, 128)] = dv[:256].astype(BF16)
            dks[:, lanes(lo, 128)] = dk[256:].astype(BF16)
            dks[:, lanes(768 + lo, 128)] = dv[256:].astype(BF16)
            return carry

        lax.fori_loop(0, 6, pair, 0)
        exchange = remote(dks, dkr.at[l], dks_sem.at[l], dkr_sem.at[l], partner)
        exchange.start()
        lt[0] = xa[l].T
        lt[1] = ctx[l].T
        exchange.wait()
        pga[:, 768:] = (pga[:, 768:].astype(F32) + dkr[l].astype(F32)).astype(BF16)
        smo[8 + 2 * l : 9 + 2 * l, :] = jnp.sum(pga[:, :768].astype(F32), axis=0, keepdims=True)
        smo[9 + 2 * l : 10 + 2 * l, :] = jnp.sum(pga[:, 1536:].astype(F32), axis=0, keepdims=True)
        dxs[...] = mm_t(pga[...], wq[l])
        hg = norm_back(s, g)

        def grads():
            for n in range(4):
                slot = n % 2
                if len(pb_copies) >= 2:
                    pb_copies[-2].wait()

                def step(i, carry):
                    if n < 3:
                        out = mm(lt[0], pga[:, lanes(768 * n + 256 * i, 256)])
                    else:
                        out = mm(lt[1], gbuf[s, :, lanes(256 * i, 256)])
                    pb[slot, :, :, :, lanes(256 * i, 256)] = out.astype(BF16).reshape(4, 2, 96, 256)
                    return carry

                lax.fori_loop(0, 3, step, 0)
                copy = pltpu.make_async_copy(
                    pb.at[slot], pao.at[l, :, :, :, pl.ds(768 * n, 768)], pb_sem.at[slot]
                )
                copy.start()
                pb_copies.append(copy)

        return hg, grads

    hg, grads = attn_back(1)
    gbuf[1] = hg.astype(BF16)
    sent2 = push_all(gbuf.at[1], g2o, 2)
    grads()

    g = gbuf[1].astype(F32)
    g_first = (g * is_first).astype(BF16)
    g_second = (g[192:256] * is_second[192:256]).astype(BF16)
    sum_first = jnp.sum(g_first.astype(F32), axis=0, keepdims=True)
    sum_second = jnp.sum(g_second.astype(F32), axis=0, keepdims=True)
    smo[26:27, :] = jnp.where(k == 0, sum_first, 0.0)
    smo[27:28, :] = jnp.where(k == 0, sum_second, sum_first)
    loads["u3"].wait()
    loads["d3"].wait()
    dxs[...] = ffn_back(g_first, k, k, act, dg1)
    dxs[192:256, :] = dxs[192:256, :] + ffn_back(g_second, 1, 1, acts, dg1s)
    gbuf[0] = norm_back(1, gbuf[1]).astype(BF16)

    hg, grads = attn_back(0)
    hbuf[0] = hg.astype(BF16)
    fsend_a = remote(hbuf.at[4], full.at[k], fs_sem, fr_sem, partner)
    fsend_b = remote(hbuf.at[0], full.at[k], fs_sem, fr_sem, partner)

    @pl.when(k == 1)
    def _():
        fsend_a.start()
        full[1] = hbuf[0]

    @pl.when(k == 0)
    def _():
        fsend_b.start()
        full[0] = hbuf[4]

    grads()
    fsend_a.wait()

    spot = lax.broadcasted_iota(jnp.int32, (128, 128), 0)
    col = lax.broadcasted_iota(jnp.int32, (128, 128), 1)
    everything = full[...].reshape(512, 768)
    for d in range(4):
        target = (seg + d) % 4
        at = spot + 128 * target
        code = ((col == 16 + at // 32) | (col == 32 + at % 32)).astype(F32).astype(BF16)
        pick = (mm_t(code, ohv[...]) > 1.5).astype(F32).astype(BF16)
        pieces[d] = mm(pick, everything).astype(BF16)
        if d > 0:
            remote(
                pieces.at[d], comb.at[k, x], us_sem.at[d], ur_sem.at[k, x], (target, 2 * z + y)
            ).start()
        else:
            far = remote(pieces.at[0], comb.at[k, x], us_sem.at[0], ur_sem.at[k, x], partner)
            near = pltpu.make_async_copy(pieces.at[0], comb.at[k, x], us_sem.at[0])

            @pl.when(k == y)
            def _():
                near.start()

            @pl.when(k != y)
            def _():
                far.start()

    for d in range(4):
        if d > 0:
            remote(
                pieces.at[d], comb.at[k, x], us_sem.at[d], ur_sem.at[k, x], partner
            ).wait_send()
        else:
            @pl.when(k == y)
            def _():
                near.wait()

            @pl.when(k != y)
            def _():
                far.wait_send()

    for j in range(2):
        for m in range(2):
            @pl.when(jnp.logical_not((2 * k + m == seg) & (j == k)))
            def _():
                remote(
                    pieces.at[0], comb.at[j, m], us_sem.at[0], ur_sem.at[j, m], partner
                ).wait_recv()

    for local, copies in (sent1, sent3, sent2):
        local.wait()
        for copy in copies:
            copy.wait()
    for copy in pb_copies[-2:]:
        copy.wait()


def run_chain(tok, cot, oh, gb, sm, ub, wq, wo, wu, wd):
    any_ = pl.BlockSpec(memory_space=pl.ANY)
    vm = pl.BlockSpec(memory_space=pltpu.VMEM)
    dma = pltpu.SemaphoreType.DMA
    shape = jax.ShapeDtypeStruct
    return pl.pallas_call(
        chain_kernel,
        out_shape=(
            shape((4, 256, 768), BF16),
            shape((4, 256, 768), BF16),
            shape((4, 256, 768), BF16),
            shape((4, 256, 768), BF16),
            shape((2, 4, 2, 96, 3072), BF16),
            shape((2, 2, 128, 768), BF16),
            shape((32, 768), F32),
        ),
        in_specs=[any_, any_, any_, vm, vm, vm, any_, any_, any_, any_],
        out_specs=(any_, any_, any_, any_, any_, any_, vm),
        scratch_shapes=[
            pltpu.VMEM((2, 768, 2304), BF16),
            pltpu.VMEM((2, 768, 768), BF16),
            pltpu.VMEM((2, 768, 3072), BF16),
            pltpu.VMEM((2, 3072, 768), BF16),
            pltpu.VMEM((5, 256, 768), BF16),
            pltpu.VMEM((2, 256, 768), BF16),
            pltpu.VMEM((2, 256, 2304), BF16),
            pltpu.VMEM((2, 256, 1536), BF16),
            pltpu.VMEM((2, 256, 768), BF16),
            pltpu.VMEM((2, 12, 512, 256), BF16),
            pltpu.VMEM((512, 256), F32),
            pltpu.VMEM((256, 768), BF16),
            pltpu.VMEM((256, 768), BF16),
            pltpu.VMEM((256, 3072), BF16),
            pltpu.VMEM((64, 3072), BF16),
            pltpu.VMEM((256, 3072), BF16),
            pltpu.VMEM((64, 3072), BF16),
            pltpu.VMEM((256, 3072), BF16),
            pltpu.VMEM((4, 256, 768), BF16),
            pltpu.VMEM((256, 768), BF16),
            pltpu.VMEM((256, 2304), BF16),
            pltpu.VMEM((256, 1536), BF16),
            pltpu.VMEM((2, 256, 1536), BF16),
            pltpu.VMEM((2, 768, 256), BF16),
            pltpu.VMEM((2, 4, 2, 96, 768), BF16),
            pltpu.VMEM((256, 768), F32),
            pltpu.VMEM((2, 256, 768), BF16),
            pltpu.VMEM((4, 128, 768), BF16),
            pltpu.VMEM((4, 8, 768), F32),
            pltpu.VMEM((512, 128), BF16),
            dma((10,)), dma((2,)), dma((3,)), dma((3,)), dma((2,)), dma((2,)),
            dma((2,)), dma((2,)), dma((2,)), dma((2,)), dma((2,)),
            dma((2,)), dma((2,)), dma((3, 3)), dma((3, 3)), dma((3,)), dma((2,)),
            dma(()), dma(()), dma((4,)), dma((2, 2)), dma(()),
        ],
        compiler_params=pltpu.CompilerParams(
            collective_id=0, has_side_effects=True, vmem_limit_bytes=62 * MIB
        ),
    )(tok, cot, oh, gb, sm, ub, wq, wo, wu, wd)


def reduce_kernel(
    x1h, x3h, g2h, c4h, pah, ush, dsh, ubs, smi,
    upo, dno, ato, smo,
    xv, gv, xs, gs, wu, wd, av, pv, lt, pu, pd, ru, rd, ao, ar, eu, ed,
    u1, d1, a1, u2, d2, a2, fu, fd, fa, ra, ta, sacc, srecv,
    in_sem, al_sem, ars_sem, arr_sem, cs_sem, cr_sem, s1_sem, r1_sem, s2_sem, r2_sem,
    us_sem, ur_sem, ul_sem, ds_sem, dr_sem, ps_sem, pr_sem, fs_sem, fr_sem, fl_sem,
    ss_sem, sr_sem,
):
    seg, dp, z, k, y, x = places()
    other = 1 - k
    partner = (seg, 2 * z + other)
    zp, zm, z2 = (z + 1) % 4, (z + 3) % 4, (z + 2) % 4
    up_z, down_z, far_z = (seg, 2 * zp + k), (seg, 2 * zm + k), (seg, 2 * z2 + k)

    def peer(d):
        return ((seg + d) % 4, dp)

    def remote(src, dst, ssem, rsem, where):
        return pltpu.make_async_remote_copy(
            src_ref=src, dst_ref=dst, send_sem=ssem, recv_sem=rsem,
            device_id=where, device_id_type=MESH,
        )

    def local(src, dst, sem):
        return pltpu.make_async_copy(src, dst, sem)

    loads = {}

    def load(name, src, dst):
        copy = local(src, dst, in_sem.at[len(loads)])
        copy.start()
        loads[name] = copy

    load("x3", x3h, xv.at[0])
    load("u2", ush.at[2], wu.at[2])
    load("c4", c4h, gv.at[0])
    load("d2", dsh.at[2], wd.at[2])

    barrier = pltpu.get_barrier_semaphore()
    for d in range(4):
        for c in range(2):
            if d == 0 and c == 1:
                continue
            where = partner if d == 0 else ((seg + d) % 4, 2 * z + c)
            pl.semaphore_signal(barrier, inc=1, device_id=where, device_id_type=MESH)
    for where in (up_z, down_z, far_z):
        pl.semaphore_signal(barrier, inc=1, device_id=where, device_id_type=MESH)
    pl.semaphore_wait(barrier, 10)

    att = []
    for l in (1, 0):
        here = local(pah.at[l, :, k], ao.at[l], al_sem.at[l])
        there = remote(pah.at[l, :, other], ar.at[l], ars_sem.at[l], arr_sem.at[l], partner)
        here.start()
        there.start()
        att.append((l, here, there))
    load("x1", x1h, xv.at[1])
    load("g2", g2h, gv.at[1])
    for e in range(2):
        load(f"u{e}", ush.at[e], wu.at[e])
        load(f"d{e}", dsh.at[e], wd.at[e])

    small_partners = (
        partner,
        (seg + 1 - 2 * x, dp),
        ((seg + 2) % 4, dp),
        (seg, 2 * (z + 1 - 2 * (z % 2)) + k),
        far_z,
    )
    smalls = [
        remote(sacc.at[i], srecv.at[i], ss_sem.at[i], sr_sem.at[i], small_partners[i])
        for i in range(5)
    ]
    sacc[0] = smi[...]
    smalls[0].start()

    def small_step(i):
        smalls[i].wait()
        total = sacc[i] + srecv[i]
        if i == 4:
            smo[...] = total
        else:
            sacc[i + 1] = total
            smalls[i + 1].start()

    def wgrad(u, e, xin, gin, rows):
        size = min(rows, 256)

        def step(r, carry):
            at = pl.ds(pl.multiple_of(size * r, size), size)
            xr = xin(at)
            pre = mm(xr, wu[e]) + ubs[e]
            a, slope = gelu_both(pre)
            av[at, :] = a.astype(BF16)
            pv[at, :] = (mm_t(gin(at), wd[e]) * slope).astype(BF16)
            lane_at = pl.ds(pl.multiple_of(size * r, size), size)
            lt[0, :, lane_at] = xr.T
            lt[1, :, lane_at] = av[at, :].T
            return carry

        lax.fori_loop(0, rows // size, step, 0)
        everything = pl.ds(0, rows)

        def out(n, carry):
            at = pl.ds(pl.multiple_of(256 * n, 256), 256)
            pu[u, :, :, :, at] = (
                mm(lt[0, :, :rows], pv[everything, at]).astype(BF16).reshape(4, 2, 96, 256)
            )
            pd[u, :, :, at] = (
                mm(lt[1, :, :rows], gin((everything, at))).astype(BF16).reshape(4, 192, 256)
            )
            return carry

        lax.fori_loop(0, 3, out, 0)
        half = pl.ds(pl.multiple_of(384 * other, 128), 384)
        copies = (
            remote(pu.at[u, :, other], ru.at[u], cs_sem.at[u, 0], cr_sem.at[u, 0], partner),
            remote(pd.at[u, :, :, half], rd.at[u], cs_sem.at[u, 1], cr_sem.at[u, 1], partner),
        )
        for copy in copies:
            copy.start()
        return copies

    own_half = pl.ds(pl.multiple_of(384 * k, 128), 384)

    class Unit:
        def __init__(self, i, shards, first, second):
            self.shards, self.first, self.second, self.i = shards, first, second, i
            rows = shards.shape[1]
            lo, hi = pl.ds(0, rows // 2), pl.ds(rows // 2, rows // 2)
            self.lo, self.hi = lo, hi
            e, f, s = shards, first, second
            self.early = [
                remote(e.at[z2, lo], f.at[0], s1_sem.at[i, 0], r1_sem.at[i, 0], up_z),
                remote(e.at[z2, hi], f.at[1], s1_sem.at[i, 1], r1_sem.at[i, 1], down_z),
                remote(e.at[zp, hi], s.at[0, hi], s1_sem.at[i, 2], r1_sem.at[i, 2], up_z),
                remote(e.at[zm, lo], s.at[1, lo], s1_sem.at[i, 3], r1_sem.at[i, 3], down_z),
            ]
            self.late = [
                remote(e.at[zp, lo], s.at[0, lo], s2_sem.at[i, 0], r2_sem.at[i, 0], up_z),
                remote(e.at[zm, hi], s.at[1, hi], s2_sem.at[i, 1], r2_sem.at[i, 1], down_z),
            ]

        def begin(self):
            for copy in self.early:
                copy.start()

        def turn(self):
            e, f = self.shards, self.first
            self.early[0].wait_recv()
            e[zp, self.lo] = (e[zp, self.lo].astype(F32) + f[0].astype(F32)).astype(BF16)
            self.late[0].start()
            self.early[1].wait_recv()
            e[zm, self.hi] = (e[zm, self.hi].astype(F32) + f[1].astype(F32)).astype(BF16)
            self.late[1].start()

        def finish(self):
            self.early[2].wait_recv()
            self.early[3].wait_recv()
            for copy in self.late:
                copy.wait_recv()
            s = self.second
            return self.shards[z].astype(F32) + (s[0].astype(F32) + s[1].astype(F32))

        def close(self):
            for copy in self.early + self.late:
                copy.wait_send()

    att_units = {l: Unit(l, ao.at[l], a1.at[l], a2.at[l]) for l in range(2)}
    up_units = {e: Unit(2 + e, eu.at[e], u1.at[e], u2.at[e]) for e in range(3)}
    down_units = {e: Unit(5 + e, ed.at[e], d1.at[e], d2.at[e]) for e in range(3)}
    tails = []

    def give_up(e):
        fu[e] = up_units[e].finish().astype(BF16)
        here = local(fu.at[e], upo.at[seg, e], ul_sem.at[e])
        here.start()
        copies = [
            remote(fu.at[e], upo.at[seg, e], us_sem.at[e, d - 1], ur_sem.at[e, d - 1], peer(d))
            for d in (1, 2, 3)
        ]
        for copy in copies:
            copy.start()

        def close():
            here.wait()
            for copy in copies:
                copy.wait()

        tails.append(close)

    def give_down(e):
        fd[e] = down_units[e].finish().astype(BF16)
        spot = dno.at[e, pl.ds(pl.multiple_of(192 * x, 64), 192), own_half]
        near = local(fd.at[e], spot, ds_sem.at[e, 0])

        def send(d):
            where = partner if d == 0 else ((seg + d) % 4, 2 * z + y)
            return remote(fd.at[e], spot, ds_sem.at[e, d], dr_sem.at[e, k, x], where)

        for d in (1, 2, 3):
            send(d).start()

        @pl.when(k == y)
        def _():
            near.start()

        @pl.when(k != y)
        def _():
            send(0).start()

        def close():
            for d in (1, 2, 3):
                send(d).wait_send()

            @pl.when(k == y)
            def _():
                near.wait()

            @pl.when(k != y)
            def _():
                send(0).wait_send()

            for j in range(2):
                for m in range(2):
                    @pl.when(jnp.logical_not((2 * k + m == seg) & (j == k)))
                    def _():
                        remote(
                            fd.at[e], spot, ds_sem.at[e, 0], dr_sem.at[e, j, m], partner
                        ).wait_recv()

        tails.append(close)

    plane = {}

    def spread_att(l):
        fa[l] = att_units[l].finish().astype(BF16)
        copies = []
        for d in (1, 2, 3):
            piece = pl.ds(pl.multiple_of(768 * ((seg + d) % 4), 128), 768)
            copies.append(
                remote(
                    fa.at[l, :, piece], ra.at[l, d - 1], ps_sem.at[l, d - 1], pr_sem.at[l, d - 1],
                    peer(d),
                )
            )
            copies[-1].start()
        plane[l] = copies

    def give_att(l):
        for copy in plane[l]:
            copy.wait()
        piece = pl.ds(pl.multiple_of(768 * seg, 128), 768)
        total = fa[l, :, piece].astype(F32) + ra[l, 0].astype(F32)
        total = total + ra[l, 1].astype(F32) + ra[l, 2].astype(F32)
        ta[l] = total.astype(BF16)
        spot = ato.at[l, :, piece]
        here = local(ta.at[l], spot, fl_sem.at[l])
        here.start()
        copies = [
            remote(ta.at[l], spot, fs_sem.at[l, d - 1], fr_sem.at[l, d - 1], peer(d))
            for d in (1, 2, 3)
        ]
        for copy in copies:
            copy.start()

        def close():
            here.wait()
            for copy in copies:
                copy.wait()

        tails.append(close)

    for name in ("x3", "u2", "c4", "d2"):
        loads[name].wait()

    def rows_of(ref, slot):
        def read(at):
            return ref[slot, at[0], at[1]] if isinstance(at, tuple) else ref[slot, at, :]

        return read

    w3 = wgrad(0, 2, rows_of(xv, 0), rows_of(gv, 0), 1024)

    for l, here, there in att:
        here.wait()
        there.wait()

        def add(i, carry):
            ao[l, i] = (ao[l, i].astype(F32) + ar[l, i].astype(F32)).astype(BF16)
            return carry

        lax.fori_loop(0, 4, add, 0)
        att_units[l].begin()
    small_step(0)

    for copy in w3:
        copy.wait()
    eu[2] = (pu[0, :, k].astype(F32) + ru[0].astype(F32)).astype(BF16)
    ed[2] = (pd[0, :, :, own_half].astype(F32) + rd[0].astype(F32)).astype(BF16)
    up_units[2].begin()
    down_units[2].begin()

    for name in ("x1", "g2", "u0", "u1", "d0", "d1"):
        loads[name].wait()
    spots = lax.broadcasted_iota(jnp.int32, (256, 1), 0)
    is_first = ((spots < PATCHES) | (k == 1)).astype(F32)
    is_second = ((spots >= PATCHES) & (k == 0)).astype(F32)
    for r in range(4):
        grad = gv[1, 256 * r : 256 * (r + 1), :].astype(F32)
        gs[64 * r : 64 * (r + 1), :] = (grad[192:] * is_second[192:]).astype(BF16)
        gv[1, 256 * r : 256 * (r + 1), :] = (grad * is_first).astype(BF16)
        xs[64 * r : 64 * (r + 1), :] = xv[1, 256 * r + 192 : 256 * (r + 1), :]
    wp = wgrad(1, k, rows_of(xv, 1), rows_of(gv, 1), 1024)
    small_step(1)
    for l in (1, 0):
        att_units[l].turn()
    up_units[2].turn()
    down_units[2].turn()

    def whole(ref):
        def read(at):
            return ref[at[0], at[1]] if isinstance(at, tuple) else ref[at, :]

        return read

    wq = wgrad(2, 1, whole(xs), whole(gs), 256)
    small_step(2)
    for copy in wp + wq:
        copy.wait()
    first = k == 0
    eu[0] = jnp.where(first, pu[1, :, k], ru[1])
    ed[0] = jnp.where(first, pd[1, :, :, own_half], rd[1])
    up_units[0].begin()
    down_units[0].begin()
    eu[1] = jnp.where(
        first,
        pu[2, :, k].astype(F32) + ru[1].astype(F32),
        pu[1, :, k].astype(F32) + ru[2].astype(F32),
    ).astype(BF16)
    ed[1] = jnp.where(
        first,
        pd[2, :, :, own_half].astype(F32) + rd[1].astype(F32),
        pd[1, :, :, own_half].astype(F32) + rd[2].astype(F32),
    ).astype(BF16)
    up_units[1].begin()
    down_units[1].begin()

    spread_att(1)
    spread_att(0)
    give_up(2)
    give_down(2)
    small_step(3)
    for e in (0, 1):
        up_units[e].turn()
        down_units[e].turn()
    give_att(1)
    give_att(0)
    small_step(4)
    for e in (0, 1):
        give_up(e)
        give_down(e)
    for close in tails:
        close()
    for unit in list(att_units.values()) + list(up_units.values()) + list(down_units.values()):
        unit.close()


def run_reduce(x1, x3, g2, c4, pa, us, ds, ubs, smo):
    any_ = pl.BlockSpec(memory_space=pl.ANY)
    vm = pl.BlockSpec(memory_space=pltpu.VMEM)
    dma = pltpu.SemaphoreType.DMA
    shape = jax.ShapeDtypeStruct
    return pl.pallas_call(
        reduce_kernel,
        out_shape=(
            shape((4, 3, 96, 768), BF16),
            shape((3, 384, 768), BF16),
            shape((2, 96, 3072), BF16),
            shape((32, 768), F32),
        ),
        in_specs=[any_] * 7 + [vm, vm],
        out_specs=(any_, any_, any_, vm),
        scratch_shapes=[
            pltpu.VMEM((2, 1024, 768), BF16),
            pltpu.VMEM((2, 1024, 768), BF16),
            pltpu.VMEM((256, 768), BF16),
            pltpu.VMEM((256, 768), BF16),
            pltpu.VMEM((3, 768, 768), BF16),
            pltpu.VMEM((3, 768, 768), BF16),
            pltpu.VMEM((1024, 768), BF16),
            pltpu.VMEM((1024, 768), BF16),
            pltpu.VMEM((2, 768, 1024), BF16),
            pltpu.VMEM((3, 4, 2, 96, 768), BF16),
            pltpu.VMEM((3, 4, 192, 768), BF16),
            pltpu.VMEM((3, 4, 96, 768), BF16),
            pltpu.VMEM((3, 4, 192, 384), BF16),
            pltpu.VMEM((2, 4, 96, 3072), BF16),
            pltpu.VMEM((2, 4, 96, 3072), BF16),
            pltpu.VMEM((3, 4, 96, 768), BF16),
            pltpu.VMEM((3, 4, 192, 384), BF16),
            pltpu.VMEM((3, 2, 48, 768), BF16),
            pltpu.VMEM((3, 2, 96, 384), BF16),
            pltpu.VMEM((2, 2, 48, 3072), BF16),
            pltpu.VMEM((3, 2, 96, 768), BF16),
            pltpu.VMEM((3, 2, 192, 384), BF16),
            pltpu.VMEM((2, 2, 96, 3072), BF16),
            pltpu.VMEM((3, 96, 768), BF16),
            pltpu.VMEM((3, 192, 384), BF16),
            pltpu.VMEM((2, 96, 3072), BF16),
            pltpu.VMEM((2, 3, 96, 768), BF16),
            pltpu.VMEM((2, 96, 768), BF16),
            pltpu.VMEM((5, 32, 768), F32),
            pltpu.VMEM((5, 32, 768), F32),
            dma((12,)), dma((2,)), dma((2,)), dma((2,)), dma((3, 2)), dma((3, 2)),
            dma((8, 4)), dma((8, 4)), dma((8, 2)), dma((8, 2)),
            dma((3, 3)), dma((3, 3)), dma((3,)), dma((3, 4)), dma((3, 2, 2)),
            dma((2, 3)), dma((2, 3)), dma((2, 3)), dma((2, 3)), dma((2,)),
            dma((5,)), dma((5,)),
        ],
        compiler_params=pltpu.CompilerParams(
            collective_id=1, has_side_effects=True, vmem_limit_bytes=62 * MIB
        ),
    )(x1, x3, g2, c4, pa, us, ds, ubs, smo)


def rolled_inputs(tokens, group_ids, type_ids, out_cotangent):
    rows = tokens.shape[1]
    spots = jnp.arange(rows, dtype=jnp.int32)
    starts = jnp.min(jnp.where(type_ids == 0, spots[None, :], rows), axis=1)
    tok, cot, oh = [], [], []
    lanes_at = jnp.arange(128, dtype=jnp.int32)[None, :]
    for m in range(tokens.shape[0]):
        s = starts[m]
        turn = lambda v: lax.dynamic_slice_in_dim(jnp.concatenate([v, v], 0), s, rows, 0)
        tok.append(turn(tokens[m]))
        cot.append(turn(out_cotangent[m]))
        gid = turn(group_ids[m])[:, None]
        spot = ((spots + s) % rows)[:, None]
        oh.append(
            (lanes_at == gid) | (lanes_at == 16 + spot // 32) | (lanes_at == 32 + spot % 32)
        )
    return jnp.stack(tok), jnp.stack(cot), jnp.stack(oh).astype(BF16)


def fast_device(
    tokens, group_ids, type_ids, norm_gain, norm_bias, qkv_weight, qv_bias, out_weight,
    out_bias, up_weight, up_bias, down_weight, down_bias, out_cotangent,
):
    seg = lax.axis_index("segment")
    dp = lax.axis_index("dp")
    tok, cot, oh = rolled_inputs(tokens, group_ids, type_ids, out_cotangent)
    gb = jnp.concatenate([norm_gain, norm_bias, jnp.zeros((6, D), BF16)], 0).astype(F32)
    sm = jnp.concatenate(
        [qv_bias.reshape(4, D), out_bias, jnp.zeros((2, D), BF16), down_bias,
         jnp.zeros((5, D), BF16)], 0
    ).astype(F32)
    ub = up_bias.astype(F32).reshape(36, 1, 256)
    x1, x3, g2, c4, pa, comb, smo = run_chain(
        tok, cot, oh, gb, sm, ub, qkv_weight, out_weight, up_weight, down_weight
    )
    us = lax.dynamic_slice_in_dim(up_weight.reshape(3, 768, 4, 768), 192 * seg, 192, 3)
    us = us.reshape(3, 768, 768)
    ds = lax.dynamic_slice_in_dim(down_weight.reshape(3, 4, 768, 768), 192 * seg, 192, 2)
    ds = ds.reshape(3, 768, 768)
    ubs = lax.dynamic_slice_in_dim(up_bias.reshape(3, 4, 768), 192 * seg, 192, 2)
    ubs = ubs.reshape(3, 1, 768).astype(F32)
    x1, x3, g2, c4 = (v.reshape(1024, 768) for v in (x1, x3, g2, c4))
    up, down, att, sm_all = run_reduce(x1, x3, g2, c4, pa, us, ds, ubs, smo)
    up = jnp.moveaxis(up.reshape(4, 3, 96, 4, 192), 0, 3).reshape(3, 96, 3072).astype(F32)
    cut = lambda v, n, ax: lax.dynamic_slice_in_dim(v, dp * n, n, ax)
    mine = cut(sm_all, 96, 1)
    upb = cut(sm_all[14:26].reshape(3, 3072), 384, 1)
    return (
        comb[0],
        comb[1].astype(F32),
        lax.dynamic_slice_in_dim(mine, seg, 1, 0),
        lax.dynamic_slice_in_dim(mine, 4 + seg, 1, 0),
        att[:, :, :2304].astype(F32),
        mine[8:12].reshape(2, 2, 96),
        att[:, :, 2304:].astype(F32),
        mine[12:14],
        up,
        upb,
        down.astype(F32),
        mine[26:29],
    )


def solution(mesh):
    known = mesh.shape["segment"] == 4 and mesh.shape["dp"] == 8
    return jax.shard_map(
        fast_device if known else per_device,
        mesh=mesh,
        in_specs=(
            P("dp", None, None),
            P("dp", None),
            P("dp", None),
            P("segment", None),
            P("segment", None),
            P(),
            P(),
            P(),
            P(),
            P(),
            P(),
            P(),
            P(),
            P("dp", None, None),
        ),
        out_specs=(
            P("dp", "segment", None),
            P("dp", "segment", None),
            P("segment", "dp"),
            P("segment", "dp"),
            P(None, "dp", None),
            P(None, None, "dp"),
            P(None, "dp", None),
            P(None, "dp"),
            P(None, "dp", None),
            P(None, "dp"),
            P(None, "dp", None),
            P(None, "dp"),
        ),
        check_vma=False,
    )
```
